512 devices in a mesh: frac: 8 (over y, core), tile: 64 (over x, z).
Axes of the slice: x: 4, y: 4, z: 16, core: 2. Of those that a mesh axis runs over, the one named last changes fastest.
Arguments:
- frames: bfloat16 [8, 2048, 4096], P('frac', 'tile'), may hold values from -6 to 6
- gain_reference: bfloat16 [2048, 4096], P('tile'), may hold values from 0.5 to 2
- defect_pixel: int32 [32768], P('tile'), may hold values from 0 to 131071, as said below
- defect_offset: int32 [32768], P('tile'), may hold values from -4 to 4, as said below
- fraction_group: int32 [8], replicated, may hold values from 0 to 7
- exposure_filter: float32 [8, 512, 512], P(None, 'tile'), may hold values from 0.25 to 1
Outputs:
- summed_image: float32 [32, 512, 512], P('frac', 'tile')
The draws below stay inside these ranges and needn't reach their ends.
Inputs may be any that keep to these rules, and one draw needn't show every extreme that they name: `defect_pixel`: within one index of tile the defective pixels are distinct. `defect_offset`: never 0; every fill source lies inside the frame.
All inputs are finite; a program needn't handle non-finite values.
Results may differ from the reference program's by a relative error of at most 0.0065.
Values may be sent and summed in bfloat16 or wider, within the bound.
No kernel may reach another device: no remote copies, remote signals or barrier semaphores. Data moves between devices by JAX's collectives and lax.ppermute only.
A program may use at most 64 MiB of HBM per device.

```python
import math
import jax
import jax.numpy as jnp
from jax import lax

P_SIZE = 512
PCOLS = 8
ROWS_DEV = 32
RIM = 4
DEF_DEV = 512
GROUPS = 8
FRACTIONS = 8
ROWS = 2048
WIDTH = 4096
PROWS = 4
PATCHES = 32
DEFECTS = 32768
N_TILE = 64


def defect_layout(key):
    stripe = ROWS_DEV * WIDTH
    keys = jax.random.split(key, 3)
    tile_keys = jax.random.split(keys[0], N_TILE)
    shuffled = jax.vmap(lambda single: jax.random.permutation(single, stripe)[:DEF_DEV])(tile_keys)
    pixel = (shuffled + (stripe - 1 - shuffled[:, :1])) % stripe
    distance = jax.random.randint(keys[1], (N_TILE, DEF_DEV), 1, RIM + 1)
    direction = 2 * jax.random.randint(keys[2], (N_TILE, DEF_DEV), 0, 2) - 1
    position = jnp.arange(DEF_DEV, dtype=jnp.int32)[None, :]
    distance = jnp.where(position < 2, RIM, distance)
    direction = jnp.where(position == 0, 1, jnp.where(position == 1, -1, direction))
    offset = direction * distance
    global_row = jnp.arange(N_TILE, dtype=jnp.int32)[:, None] * ROWS_DEV + pixel // WIDTH
    target = global_row + offset
    offset = jnp.where((target < 0) | (target >= ROWS_DEV * N_TILE), -offset, offset)
    return (pixel.reshape(-1).astype(jnp.int32), offset.reshape(-1).astype(jnp.int32))


def draw_defect_pixel(key, part):
    shared = defect_layout(key)
    return shared[0]


def draw_defect_offset(key, part):
    shared = defect_layout(key)
    return shared[1]


def set_ends(result, stream_key, least, high):
    longest = result.shape.index(max(result.shape))
    spots = []
    for shift in (0, 1):
        where = [jax.random.randint(jax.random.fold_in(stream_key, axis), (), 0, length) for axis, length in enumerate(result.shape)]
        where[longest] = (where[longest] + shift) % result.shape[longest]
        spots.append(tuple(where))
    return result.at[spots[0]].set(least).at[spots[1]].set(high)


def block_scale(stream_key, dims, shards, smallest, high):
    loudness = 1.0
    for dim, blocks in shards:
        steps = jax.random.uniform(jax.random.fold_in(jax.random.fold_in(stream_key, 6), dim), (blocks,), jnp.float32, smallest / len(shards), high / len(shards))
        loudness = loudness * jnp.repeat(jnp.exp(steps), dims[dim] // blocks).reshape((-1,) + (1,) * (len(dims) - 1 - dim))
    return loudness


def scatter_about(stream_key, shape, scale, most, pieces=(), kind=jnp.bfloat16):
    drawn = jax.random.normal(stream_key, shape, jnp.float32) * scale
    if len(pieces) > 0:
        drawn = block_scale(stream_key, shape, pieces, -0.22, 0.18) * drawn
    return jnp.clip(drawn, min=-most, max=most).astype(kind)


def setup_inputs(seed: int = 0) -> dict:
    arg_keys = jax.random.split(jax.random.key(seed), 7)
    return {
        "frames": scatter_about(arg_keys[0], (FRACTIONS, ROWS, WIDTH), 1.0, 6.0, ((0, 8), (1, 64))),
        "gain_reference": jnp.clip(jnp.exp(math.log(2.0) - 1.3862944 * jax.random.uniform(arg_keys[1], (ROWS, WIDTH), jnp.float32) ** block_scale(arg_keys[1], (ROWS, WIDTH), ((0, 64),), -0.2, 0.2)), 0.5, 2.0).astype(jnp.bfloat16),
        "defect_pixel": draw_defect_pixel(jax.random.fold_in(arg_keys[6], 71), 0),
        "defect_offset": draw_defect_offset(jax.random.fold_in(arg_keys[6], 71), 0),
        "fraction_group": set_ends(jax.random.randint(arg_keys[4], (FRACTIONS,), 0, GROUPS), jax.random.fold_in(arg_keys[4], 1), 0, GROUPS - 1).astype(jnp.int32),
        "exposure_filter": jnp.clip(jnp.exp(math.log(1.0) - 1.3862944 * jax.random.uniform(arg_keys[5], (GROUPS, P_SIZE, P_SIZE), jnp.float32) ** block_scale(arg_keys[5], (GROUPS, P_SIZE, P_SIZE), ((1, 64),), -0.2, 0.2)), 0.25, 1.0),
    }


def dft_tables(length):
    positions = jnp.arange(length, dtype=jnp.int32)
    product = positions[:, None] * positions[None, :] % length
    angles = product.astype(jnp.float32) * (2.0 * math.pi / length)
    return (jnp.cos(angles).astype(jnp.bfloat16), jnp.sin(angles).astype(jnp.bfloat16))

def rounded(values):
    return lax.optimization_barrier(values.astype(jnp.bfloat16)).astype(jnp.float32)

def reference(frames, gain_reference, defect_pixel, defect_offset, fraction_group, exposure_filter):
    cosine, sine_table = dft_tables(P_SIZE)
    cos_wide = cosine.astype(jnp.float32)
    sin_wide = sine_table.astype(jnp.float32)
    tile_of = jnp.arange(DEFECTS, dtype=jnp.int32) // DEF_DEV
    defect_row = tile_of * ROWS_DEV + defect_pixel // WIDTH
    defect_column = defect_pixel % WIDTH
    source_row = defect_row + defect_offset
    gain_wide = gain_reference.astype(jnp.float32)

    def one_fraction(totals, inputs):
        frame_now, group_now = inputs
        corrected = frame_now.astype(jnp.float32) * gain_wide
        filled = corrected.at[defect_row, defect_column].set(corrected[source_row, defect_column])
        blocks = rounded(filled).reshape(PROWS, P_SIZE, PCOLS, P_SIZE)
        row_real = rounded(jnp.einsum('aycx,xk->ayck', blocks, cos_wide))
        row_imag = rounded(-jnp.einsum('aycx,xk->ayck', blocks, sin_wide))
        spec_real = jnp.einsum('qy,ayck->ackq', cos_wide, row_real) + jnp.einsum('qy,ayck->ackq', sin_wide, row_imag)
        spec_imag = jnp.einsum('qy,ayck->ackq', cos_wide, row_imag) - jnp.einsum('qy,ayck->ackq', sin_wide, row_real)
        weight = exposure_filter[group_now]
        return ((totals[0] + weight * spec_real, totals[1] + weight * spec_imag, totals[2] + weight * weight), None)
    start = (jnp.zeros((PROWS, PCOLS, P_SIZE, P_SIZE), jnp.float32), jnp.zeros((PROWS, PCOLS, P_SIZE, P_SIZE), jnp.float32), jnp.zeros((P_SIZE, P_SIZE), jnp.float32))
    totals, unused = lax.scan(one_fraction, start, (frames, fraction_group))
    normalizer = jnp.sqrt(totals[2])
    owned_real = rounded(totals[0] / normalizer)
    owned_imag = rounded(totals[1] / normalizer)
    back_real = rounded((jnp.einsum('ackq,yq->acky', owned_real, cos_wide) - jnp.einsum('ackq,yq->acky', owned_imag, sin_wide)) / P_SIZE)
    back_imag = rounded((jnp.einsum('ackq,yq->acky', owned_imag, cos_wide) + jnp.einsum('ackq,yq->acky', owned_real, sin_wide)) / P_SIZE)
    summed_image = (jnp.einsum('acky,xk->acyx', back_real, cos_wide) - jnp.einsum('acky,xk->acyx', back_imag, sin_wide)) / P_SIZE
    return summed_image.reshape(PATCHES, P_SIZE, P_SIZE)
```

```python
import jax
import jax.numpy as jnp
import ml_dtypes
import numpy as np
from jax import lax
from jax.experimental import pallas as pl
from jax.experimental.pallas import tpu as pltpu
from jax.sharding import PartitionSpec as P

N = 512
RIM = 4
TILES = 64
FRACS = 8
COLS = 8
ROWS = 32
WIDTH = N * COLS
F32 = jnp.float32
BF16 = jnp.bfloat16
VMEM_LIMIT = 48 * 1024 * 1024


def wave(a, b):
    angle = (2.0 * np.pi / N) * (np.multiply.outer(a, b) % N)
    return np.cos(angle), np.sin(angle)


def owned_columns():
    tile = np.arange(TILES)[:, None]
    return 8 * tile + np.arange(4)[None, :] + (tile >= TILES // 2)


def forward_columns_table():
    cosine, sine = wave(owned_columns(), np.arange(N))
    table = np.stack([cosine, -sine], axis=1)
    table[0, 1, 0] = 1.0 - 2.0 * (np.arange(N) % 2)
    return table.reshape(N, N).astype(ml_dtypes.bfloat16)


def forward_rows_table():
    cosine, sine = wave(np.arange(N), np.arange(N))
    return np.concatenate([cosine, sine], axis=1).astype(ml_dtypes.bfloat16)


def inverse_rows_table():
    rows = (8 * np.arange(TILES)[None, :] + np.arange(8)[:, None]).reshape(-1)
    cosine, sine = wave(rows, np.arange(N))
    return np.concatenate([cosine, sine], axis=0).astype(ml_dtypes.bfloat16)


def inverse_columns_table():
    cosine, sine = wave(owned_columns(), np.arange(N))
    table = np.stack([2.0 * cosine, -2.0 * sine], axis=1)
    table[0, 0, 0] = 1.0
    table[0, 1, 0] = 1.0 - 2.0 * (np.arange(N) % 2)
    table = table.transpose(2, 0, 1, 3) / N
    return table.reshape(4, 2 * TILES, N).astype(ml_dtypes.bfloat16)


def sum_and_spread_table():
    part, k, patch = np.meshgrid(np.arange(2), np.arange(4), np.arange(4), indexing="ij")
    source = (patch * 8 + part * 4 + k).reshape(-1)
    one = np.repeat(source[:, None] == np.arange(32)[None, :], 8, axis=0)
    return np.tile(one, (1, FRACS)).astype(ml_dtypes.bfloat16)


def dot(a, b, contract):
    return lax.dot_general(a, b, ((contract[:1], contract[1:]), ((), ())), preferred_element_type=F32)


def prepare_kernel(place, groups, filters, pixel, offset, fill_map, weight, flipped, first_rows):
    spot = pixel[...]
    step = offset[...].astype(F32)
    row_key = ((spot >> 7) & 31) * ROWS + (spot >> 12)
    lane_hot = (lax.broadcasted_iota(jnp.int32, (128, spot.shape[1]), 0) == (spot & 127)).astype(F32).astype(BF16)
    for part in range(4):
        rows = lax.broadcasted_iota(jnp.int32, (256, spot.shape[1]), 0) + 256 * part
        row_hot = jnp.where(rows == row_key, step, 0.0).astype(BF16)
        found = dot(row_hot, lane_hot, (1, 1)).astype(BF16)
        for i in range(8):
            lane = (part * 8 + i) * 128
            fill_map[:, lane : lane + 128] = found[i * ROWS : (i + 1) * ROWS]
    square = jnp.zeros(filters.shape[1:], F32)
    for f in range(FRACS):
        square = square + filters[groups[f]] * filters[groups[f]]
    mine = filters[groups[place[0]]] / jnp.sqrt(square)
    turn = (lax.broadcasted_iota(jnp.int32, (N, N), 0) + lax.broadcasted_iota(jnp.int32, (N, N), 1)) & (N - 1)
    turn = (turn == 0).astype(F32).astype(BF16)
    high = mine.astype(BF16)
    low = (mine - high.astype(F32)).astype(BF16)
    back = dot(high, turn, (1, 0)) + dot(low, turn, (1, 0))
    weight[...] = mine
    flipped[...] = back
    first_rows[0:1, :] = mine[0:1]
    first_rows[1:2, :] = back[0:1]


def columns_kernel(frames, gain, above, below, fill_map, table, out, extended, filled):
    for c in range(COLS):
        lanes = slice(c * N, (c + 1) * N)
        extended[8 - RIM : 8, :] = above[:, lanes].astype(F32)
        extended[8 + ROWS : 8 + ROWS + RIM, :] = below[:, lanes].astype(F32)
        value = frames[:, lanes].astype(F32) * gain[:, lanes].astype(F32)
        extended[8 : 8 + ROWS, :] = value
        wanted = fill_map[:, lanes].astype(F32)
        for step in range(-RIM, RIM + 1):
            if step != 0:
                value = jnp.where(wanted == step, extended[8 + step : 8 + step + ROWS, :], value)
        filled[c * ROWS : (c + 1) * ROWS, :] = value.astype(BF16)
    out[...] = dot(table[...], filled[...], (1, 1)).astype(BF16)


def rows_kernel(place, spectrum, weight, flipped, mirror, mirror_first, table, out, by_row, pair):
    tile = place[1]
    lower = tile < TILES // 2
    first = tile == 0
    for k in range(4):
        own = jnp.where(lower, weight[k : k + 1], weight[k + 1 : k + 2])
        if k == 0:
            other = jnp.where(lower, jnp.where(first, flipped[0:1], mirror_first[1:2]), mirror[7:8])
        else:
            other = jnp.where(lower, mirror[8 - k : 9 - k], mirror[7 - k : 8 - k])
        both = 0.5 * (own + other)
        pair[k : k + 1, :] = both
        if k == 0:
            both = jnp.where(first, 0.5 * (mirror_first[0:1] + mirror_first[1:2]), both)
        pair[4 + k : 5 + k, :] = both

    group = lax.broadcasted_iota(jnp.int32, (16, 8, 128), 2) >> 5
    source = spectrum[...].astype(F32).reshape(4, 4, 4, 8, 2 * 128)
    for half in range(2):
        pieces = []
        for j in range(4):
            piece = source[:, :, j, :, half * 128 : (half + 1) * 128].reshape(128, 128)
            pieces.append([piece if d == 0 else pltpu.roll(piece, 32 * d, 1) for d in range(4)])
        for c in range(4):
            found = pieces[3][(3 - c) % 4].reshape(16, 8, 128)
            for j in range(3):
                found = jnp.where(group == j, pieces[j][(j - c) % 4].reshape(16, 8, 128), found)
            for a in range(4):
                for quarter in range(4):
                    by_row[a * 8 + half * 4 + c, :, quarter * 128 : (quarter + 1) * 128] = found[a * 4 + quarter]
    operand = by_row[...].reshape(256, N).astype(BF16)
    scale = pair[...][None]
    with_cosine = dot(operand, table[:, :N], (1, 0)).reshape(32, 8, N) * scale
    with_sine = dot(operand, table[:, N:], (1, 0)).reshape(32, 8, N) * scale
    sign = jnp.where(lax.broadcasted_iota(jnp.int32, (1, 8, 1), 1) < 4, 1.0, -1.0)
    total = with_cosine + sign * pltpu.roll(with_sine, 4, 1)
    out[...] = total.reshape(256, N).astype(BF16)


def back_rows_kernel(parts, spread, table, out, both):
    owned = dot(spread[...], parts[...], (1, 0)).astype(BF16)
    turned = dot(table[...], owned, (1, 1))
    real = turned[:N, :128] - turned[N:, 128:]
    imag = turned[:N, 128:] + turned[N:, :128]
    row = lax.broadcasted_iota(jnp.int32, (TILES, 128), 1) & 7
    for part, value in enumerate((real, imag)):
        picked = value[:TILES]
        for y in range(1, 8):
            picked = jnp.where(row == y, value[y * TILES : (y + 1) * TILES], picked)
        both[pl.ds(part, TILES, stride=2), :] = picked * (1.0 / N)
    out[...] = both[...].astype(BF16)


def back_columns_kernel(spectrum, table, out):
    turned = spectrum[...].astype(F32).T.astype(BF16)
    image = dot(turned[:32], table[0], (1, 0))
    for k in range(1, 4):
        image = image + dot(turned[32 * k : 32 * (k + 1)], table[k], (1, 0))
    out[...] = image.reshape(4, 8, N)


def call(kernel, outs, scratch, scalars, cost, *args):
    smem = pl.BlockSpec(memory_space=pltpu.SMEM)
    vmem = pl.BlockSpec(memory_space=pltpu.VMEM)
    many = isinstance(outs, (list, tuple))
    return pl.pallas_call(
        kernel,
        out_shape=outs,
        in_specs=[smem] * scalars + [vmem] * (len(args) - scalars),
        out_specs=[vmem] * len(outs) if many else vmem,
        scratch_shapes=scratch,
        compiler_params=pltpu.CompilerParams(vmem_limit_bytes=VMEM_LIMIT),
        cost_estimate=pl.CostEstimate(flops=cost, bytes_accessed=1 << 21, transcendentals=0),
    )(*args)


def per_device(frames, gain, defect_pixel, defect_offset, fraction_group, exposure_filter):
    frames = frames.reshape(ROWS, WIDTH)
    place = jnp.stack([lax.axis_index("frac"), lax.axis_index("tile")]).astype(jnp.int32)

    def edge(rows):
        return (frames[rows].astype(F32) * gain[rows].astype(F32)).astype(BF16)

    up = [(i, i + 1) for i in range(TILES - 1)]
    above = lax.ppermute(edge(slice(ROWS - RIM, ROWS)), "tile", up)
    below = lax.ppermute(edge(slice(0, RIM)), "tile", [(b, a) for a, b in up])

    shape = jax.ShapeDtypeStruct
    fill_map, weight, flipped, first_rows = call(
        prepare_kernel,
        [shape((ROWS, WIDTH), BF16), shape((8, N), F32), shape((8, N), F32), shape((2, N), F32)],
        [],
        2,
        1 << 27,
        place,
        fraction_group,
        exposure_filter,
        defect_pixel.reshape(1, -1),
        defect_offset.reshape(1, -1),
    )
    half = TILES // 2
    mirror = lax.ppermute(flipped, "tile", [(t, TILES - 1 - t) for t in range(TILES)])
    mirror_first = lax.ppermute(
        first_rows, "tile", [(half, 0)] + [(t, TILES - t) for t in range(half + 1, TILES)]
    )

    columns = call(
        columns_kernel,
        shape((N, COLS * ROWS), BF16),
        [pltpu.VMEM((ROWS + 16, N), F32), pltpu.VMEM((COLS * ROWS, N), BF16)],
        0,
        1 << 27,
        frames,
        gain,
        above,
        below,
        fill_map,
        jnp.asarray(forward_columns_table()),
    )
    columns = lax.all_to_all(columns.reshape(TILES, 8, COLS * ROWS), "tile", 0, 0, tiled=True)

    weighted = call(
        rows_kernel,
        shape((256, N), BF16),
        [pltpu.VMEM((32, 8, N), F32), pltpu.VMEM((8, N), F32)],
        1,
        1 << 28,
        place,
        columns.reshape(N, COLS * ROWS),
        weight,
        flipped,
        mirror,
        mirror_first,
        jnp.asarray(forward_rows_table()),
    )
    parts = lax.all_to_all(weighted.reshape(FRACS, 32, N), "frac", 0, 0, tiled=True)

    back = call(
        back_rows_kernel,
        shape((2 * TILES, 128), BF16),
        [pltpu.VMEM((2 * TILES, 128), F32)],
        0,
        1 << 28,
        parts.reshape(256, N),
        jnp.asarray(sum_and_spread_table()),
        jnp.asarray(inverse_rows_table()),
    )
    back = lax.all_to_all(back.reshape(TILES, 2, 128), "tile", 0, 0, tiled=True)

    return call(
        back_columns_kernel,
        shape((4, 8, N), F32),
        [],
        0,
        1 << 26,
        back.reshape(2 * TILES, 128),
        jnp.asarray(inverse_columns_table()),
    )


def solution(mesh):
    return jax.shard_map(
        per_device,
        mesh=mesh,
        in_specs=(
            P("frac", "tile", None),
            P("tile", None),
            P("tile"),
            P("tile"),
            P(),
            P(None, "tile", None),
        ),
        out_specs=P("frac", "tile", None),
        check_vma=False,
    )
```

```python
import jax
import jax.numpy as jnp
import ml_dtypes
import numpy as np
from jax import lax
from jax.experimental import pallas as pl
from jax.experimental.pallas import tpu as pltpu
from jax.sharding import PartitionSpec as P

N = 512
RIM = 4
TILES = 64
HALF = TILES // 2
FRACS = 8
COLS = 8
ROWS = 32
WIDTH = N * COLS
F32 = jnp.float32
BF16 = jnp.bfloat16
VMEM_LIMIT = 48 * 1024 * 1024


def wave(a, b):
    angle = (2.0 * np.pi / N) * (np.multiply.outer(a, b) % N)
    return np.cos(angle), np.sin(angle)


def owned_columns():
    tile = np.arange(TILES)[:, None]
    near = np.array([1, 2, 3, 4])[None, :]
    return 8 * tile + np.where(tile < HALF, np.array([1, 2, 3, 8])[None, :], near)


def forward_columns_table():
    cosine, sine = wave(owned_columns(), np.arange(N))
    table = np.stack([cosine, -sine], axis=1)
    table[HALF - 1, 1, 3] = 1.0
    return table.reshape(N, N).astype(ml_dtypes.bfloat16)


def forward_rows_table():
    cosine, sine = wave(np.arange(N), np.arange(N))
    return np.concatenate([cosine, sine], axis=1).astype(ml_dtypes.bfloat16)


def inverse_rows_table():
    rows = (8 * np.arange(TILES)[None, :] + np.arange(8)[:, None]).reshape(-1)
    cosine, sine = wave(rows, np.arange(N))
    return np.concatenate([cosine, sine], axis=0).astype(ml_dtypes.bfloat16)


def inverse_columns_table():
    cosine, sine = wave(owned_columns(), np.arange(N))
    table = np.stack([2.0 * cosine, -2.0 * sine], axis=1)
    table[HALF - 1, 0, 3] = 1.0 - 2.0 * (np.arange(N) % 2)
    table[HALF - 1, 1, 3] = 1.0
    table = table.transpose(2, 0, 1, 3) / N
    return table.reshape(4, 2 * TILES, N).astype(ml_dtypes.bfloat16)


def sum_and_spread_table():
    part, k, patch = np.meshgrid(np.arange(2), np.arange(4), np.arange(4), indexing="ij")
    source = (patch * 8 + part * 4 + k).reshape(-1)
    one = np.repeat(source[:, None] == np.arange(32)[None, :], 8, axis=0)
    return np.tile(one, (1, FRACS)).astype(ml_dtypes.bfloat16)


def dot(a, b, contract):
    return lax.dot_general(a, b, ((contract[:1], contract[1:]), ((), ())), preferred_element_type=F32)


def weights_kernel(place, groups, filters, weight, mirror, first_rows):
    square = jnp.zeros(filters.shape[1:], F32)
    for f in range(FRACS):
        square = square + filters[groups[f]] * filters[groups[f]]
    mine = filters[groups[place[0]]] / jnp.sqrt(square)
    turn = (lax.broadcasted_iota(jnp.int32, (N, N), 0) + lax.broadcasted_iota(jnp.int32, (N, N), 1)) & (N - 1)
    turn = (turn == 0).astype(F32).astype(BF16)
    high = mine.astype(BF16)
    low = (mine - high.astype(F32)).astype(BF16)
    back = dot(high, turn, (1, 0)) + dot(low, turn, (1, 0))
    weight[...] = mine
    mirror[...] = back
    mirror[0:1, :] = mine[0:1]
    mirror[1:2, :] = back[0:1]
    first_rows[0:1, :] = mine[0:1]
    first_rows[1:2, :] = back[0:1]


def fill_kernel(pixel_in, offset_in, frames_in, gain_in, filled, edges, pixel, offset, frames, gain, fill_map, extended, sems):
    pairs = ((pixel_in, pixel), (offset_in, offset), (frames_in, frames), (gain_in, gain))
    copies = [pltpu.make_async_copy(a, b, sems.at[i]) for i, (a, b) in enumerate(pairs)]
    for copy in copies:
        copy.start()
    copies[0].wait()
    copies[1].wait()
    spot = pixel[...]
    step = offset[...].astype(F32)
    row_key = ((spot >> 7) & 31) * ROWS + (spot >> 12)
    lane_hot = (lax.broadcasted_iota(jnp.int32, (128, spot.shape[1]), 0) == (spot & 127)).astype(F32).astype(BF16)
    for part in range(4):
        rows = lax.broadcasted_iota(jnp.int32, (256, spot.shape[1]), 0) + 256 * part
        row_hot = jnp.where(rows == row_key, step, 0.0).astype(BF16)
        found = dot(row_hot, lane_hot, (1, 1))
        for i in range(8):
            lane = (part * 8 + i) * 128
            fill_map[:, lane : lane + 128] = found[i * ROWS : (i + 1) * ROWS]
    copies[2].wait()
    copies[3].wait()
    extended[0:8, :] = jnp.zeros((8, N), F32)
    extended[8 + ROWS : 16 + ROWS, :] = jnp.zeros((8, N), F32)
    for c in range(COLS):
        lanes = slice(c * N, (c + 1) * N)
        value = frames[:, lanes].astype(F32) * gain[:, lanes].astype(F32)
        extended[8 : 8 + ROWS, :] = value
        wanted = fill_map[:, lanes]
        edges[0:8, lanes] = wanted[0:8]
        edges[8:16, lanes] = wanted[ROWS - 8 : ROWS]
        for step in range(-RIM, RIM + 1):
            if step != 0:
                value = jnp.where(wanted == step, extended[8 + step : 8 + step + ROWS, :], value)
        filled[c * ROWS : (c + 1) * ROWS, :] = value.astype(BF16)


def columns_kernel(above, below, filled, edges, table, out, halo, operand):
    halo[...] = jnp.zeros(halo.shape, F32)
    halo[4:8, :] = above[...].astype(F32)
    halo[24:28, :] = below[...].astype(F32)
    for c in range(COLS):
        lanes = slice(c * N, (c + 1) * N)
        top = jnp.zeros((8, N), F32)
        bottom = jnp.zeros((8, N), F32)
        for step in range(1, RIM + 1):
            top = top + jnp.where(edges[0:8, lanes] == -step, halo[8 - step : 16 - step, lanes], 0.0)
            bottom = bottom + jnp.where(edges[8:16, lanes] == step, halo[16 + step : 24 + step, lanes], 0.0)
        rows = filled[c * ROWS : (c + 1) * ROWS, :].astype(F32)
        rows = jnp.concatenate([rows[0:8] + top, rows[8 : ROWS - 8], rows[ROWS - 8 :] + bottom], axis=0)
        operand[c * ROWS : (c + 1) * ROWS, :] = rows.astype(BF16)
    out[...] = dot(table[...], operand[...], (1, 1)).astype(BF16)


def rows_kernel(place, spectrum, weight, mirror, following, table, out, by_row, pair):
    tile = place[1]
    lower = tile < HALF
    last = tile == HALF - 1
    for k in range(4):
        if k < 3:
            own = weight[k + 1 : k + 2]
            other = mirror[7 - k : 8 - k]
        else:
            own = jnp.where(lower, following[0:1], weight[4:5])
            other = jnp.where(lower, mirror[1:2], mirror[4:5])
        both = 0.5 * (own + other)
        if k == 3:
            pair[3:4, :] = jnp.where(last, 0.5 * (mirror[0:1] + mirror[1:2]), both)
            both = jnp.where(last, 0.5 * (following[0:1] + following[1:2]), both)
        else:
            pair[k : k + 1, :] = both
        pair[4 + k : 5 + k, :] = both

    group = lax.broadcasted_iota(jnp.int32, (16, 8, 128), 2) >> 5
    source = spectrum[...].astype(F32).reshape(4, 4, 4, 8, 2 * 128)
    for half in range(2):
        pieces = []
        for j in range(4):
            piece = source[:, :, j, :, half * 128 : (half + 1) * 128].reshape(128, 128)
            pieces.append([piece if d == 0 else pltpu.roll(piece, 32 * d, 1) for d in range(4)])
        for c in range(4):
            found = pieces[3][(3 - c) % 4].reshape(16, 8, 128)
            for j in range(3):
                found = jnp.where(group == j, pieces[j][(j - c) % 4].reshape(16, 8, 128), found)
            for a in range(4):
                for quarter in range(4):
                    by_row[a * 8 + half * 4 + c, :, quarter * 128 : (quarter + 1) * 128] = found[a * 4 + quarter]
    operand = by_row[...].reshape(256, N).astype(BF16)
    scale = pair[...][None]
    with_cosine = dot(operand, table[:, :N], (1, 0)).reshape(32, 8, N) * scale
    with_sine = dot(operand, table[:, N:], (1, 0)).reshape(32, 8, N) * scale
    sign = jnp.where(lax.broadcasted_iota(jnp.int32, (1, 8, 1), 1) < 4, 1.0, -1.0)
    total = with_cosine + sign * pltpu.roll(with_sine, 4, 1)
    out[...] = total.reshape(256, N).astype(BF16)


def back_rows_kernel(parts, spread, table, out, both):
    owned = dot(spread[...], parts[...], (1, 0)).astype(BF16)
    turned = dot(table[...], owned, (1, 1))
    real = turned[:N, :128] - turned[N:, 128:]
    imag = turned[:N, 128:] + turned[N:, :128]
    row = lax.broadcasted_iota(jnp.int32, (TILES, 128), 1) & 7
    for part, value in enumerate((real, imag)):
        picked = value[:TILES]
        for y in range(1, 8):
            picked = jnp.where(row == y, value[y * TILES : (y + 1) * TILES], picked)
        both[pl.ds(part, TILES, stride=2), :] = picked * (1.0 / N)
    out[...] = both[...].astype(BF16)


def back_columns_kernel(spectrum, table, out):
    turned = spectrum[...].astype(F32).T.astype(BF16)
    image = dot(turned[:32], table[0], (1, 0))
    for k in range(1, 4):
        image = image + dot(turned[32 * k : 32 * (k + 1)], table[k], (1, 0))
    out[...] = image.reshape(4, 8, N)


def call(kernel, outs, scratch, scalars, cost, *args, space=pltpu.VMEM):
    smem = pl.BlockSpec(memory_space=pltpu.SMEM)
    vmem = pl.BlockSpec(memory_space=pltpu.VMEM)
    many = isinstance(outs, (list, tuple))
    return pl.pallas_call(
        kernel,
        out_shape=outs,
        in_specs=[smem] * scalars + [pl.BlockSpec(memory_space=space)] * (len(args) - scalars),
        out_specs=[vmem] * len(outs) if many else vmem,
        scratch_shapes=scratch,
        compiler_params=pltpu.CompilerParams(vmem_limit_bytes=VMEM_LIMIT),
        cost_estimate=pl.CostEstimate(flops=cost, bytes_accessed=1 << 21, transcendentals=0),
    )(*args)


def per_device(frames, gain, defect_pixel, defect_offset, fraction_group, exposure_filter):
    frames = frames.reshape(ROWS, WIDTH)
    place = jnp.stack([lax.axis_index("frac"), lax.axis_index("tile")]).astype(jnp.int32)

    def edge(rows):
        return (frames[rows].astype(F32) * gain[rows].astype(F32)).astype(BF16)

    up = [(i, i + 1) for i in range(TILES - 1)]
    above = lax.ppermute(edge(slice(ROWS - RIM, ROWS)), "tile", up)
    below = lax.ppermute(edge(slice(0, RIM)), "tile", [(b, a) for a, b in up])

    shape = jax.ShapeDtypeStruct
    weight, mirror, first_rows = call(
        weights_kernel,
        [shape((8, N), F32), shape((8, N), F32), shape((2, N), F32)],
        [],
        2,
        1 << 23,
        place,
        fraction_group,
        exposure_filter,
    )
    mirror = lax.ppermute(mirror, "tile", [(t, TILES - 1 - t) for t in range(TILES)])
    following = lax.ppermute(first_rows, "tile", [((t + 1) % HALF, t) for t in range(HALF)])

    defects = defect_pixel.shape[0]
    filled, edges = call(
        fill_kernel,
        [shape((COLS * ROWS, N), BF16), shape((16, WIDTH), F32)],
        [
            pltpu.VMEM((1, defects), jnp.int32),
            pltpu.VMEM((1, defects), jnp.int32),
            pltpu.VMEM((ROWS, WIDTH), BF16),
            pltpu.VMEM((ROWS, WIDTH), BF16),
            pltpu.VMEM((ROWS, WIDTH), F32),
            pltpu.VMEM((ROWS + 16, N), F32),
            pltpu.SemaphoreType.DMA((4,)),
        ],
        0,
        1 << 27,
        defect_pixel.reshape(1, -1),
        defect_offset.reshape(1, -1),
        frames,
        gain,
        space=pltpu.HBM,
    )
    columns = call(
        columns_kernel,
        shape((N, COLS * ROWS), BF16),
        [pltpu.VMEM((32, WIDTH), F32), pltpu.VMEM((COLS * ROWS, N), BF16)],
        0,
        1 << 27,
        above,
        below,
        filled,
        edges,
        jnp.asarray(forward_columns_table()),
    )
    columns = lax.all_to_all(columns.reshape(TILES, 8, COLS * ROWS), "tile", 0, 0, tiled=True)

    weighted = call(
        rows_kernel,
        shape((256, N), BF16),
        [pltpu.VMEM((32, 8, N), F32), pltpu.VMEM((8, N), F32)],
        1,
        1 << 28,
        place,
        columns.reshape(N, COLS * ROWS),
        weight,
        mirror,
        following,
        jnp.asarray(forward_rows_table()),
    )
    parts = lax.all_to_all(weighted.reshape(FRACS, 32, N), "frac", 0, 0, tiled=True)

    back = call(
        back_rows_kernel,
        shape((2 * TILES, 128), BF16),
        [pltpu.VMEM((2 * TILES, 128), F32)],
        0,
        1 << 28,
        parts.reshape(256, N),
        jnp.asarray(sum_and_spread_table()),
        jnp.asarray(inverse_rows_table()),
    )
    back = lax.all_to_all(back.reshape(TILES, 2, 128), "tile", 0, 0, tiled=True)

    return call(
        back_columns_kernel,
        shape((4, 8, N), F32),
        [],
        0,
        1 << 26,
        back.reshape(2 * TILES, 128),
        jnp.asarray(inverse_columns_table()),
    )


def solution(mesh):
    return jax.shard_map(
        per_device,
        mesh=mesh,
        in_specs=(
            P("frac", "tile", None),
            P("tile", None),
            P("tile"),
            P("tile"),
            P(),
            P(None, "tile", None),
        ),
        out_specs=P("frac", "tile", None),
        check_vma=False,
    )
```

```python
import jax
import jax.numpy as jnp
import ml_dtypes
import numpy as np
from jax import lax
from jax.experimental import pallas as pl
from jax.experimental.pallas import tpu as pltpu
from jax.sharding import PartitionSpec as P

N = 512
RIM = 4
MARK = 64.0
TILES = 64
HALF = TILES // 2
FRACS = 8
COLS = 8
ROWS = 32
WIDTH = N * COLS
F32 = jnp.float32
BF16 = jnp.bfloat16
VMEM_LIMIT = 48 * 1024 * 1024


def wave(a, b):
    angle = (2.0 * np.pi / N) * (np.multiply.outer(a, b) % N)
    return np.cos(angle), np.sin(angle)


def owned_columns():
    tile = np.arange(TILES)[:, None]
    near = np.array([1, 2, 3, 4])[None, :]
    return 8 * tile + np.where(tile < HALF, np.array([1, 2, 3, 8])[None, :], near)


def forward_columns_table():
    cosine, sine = wave(owned_columns(), np.arange(N))
    table = np.stack([cosine, -sine], axis=1)
    table[HALF - 1, 1, 3] = 1.0
    return table.reshape(N, N).astype(ml_dtypes.bfloat16)


def forward_rows_table():
    cosine, sine = wave((np.arange(N) + RIM) % N, np.arange(N))
    return np.concatenate([cosine, sine], axis=1).astype(ml_dtypes.bfloat16)


def inverse_rows_table():
    rows = (8 * np.arange(TILES)[None, :] + np.arange(8)[:, None]).reshape(-1)
    cosine, sine = wave(rows, np.arange(N))
    return np.concatenate([cosine, sine], axis=0).astype(ml_dtypes.bfloat16)


def inverse_columns_table():
    cosine, sine = wave(owned_columns(), np.arange(N))
    table = np.stack([2.0 * cosine, -2.0 * sine], axis=1)
    table[HALF - 1, 0, 3] = 1.0 - 2.0 * (np.arange(N) % 2)
    table[HALF - 1, 1, 3] = 1.0
    table = table.transpose(2, 0, 1, 3) / N
    return table.reshape(4, 2 * TILES, N).astype(ml_dtypes.bfloat16)


def sum_and_spread_table():
    part, k, patch = np.meshgrid(np.arange(2), np.arange(4), np.arange(4), indexing="ij")
    source = (patch * 8 + part * 4 + k).reshape(-1)
    one = np.repeat(source[:, None] == np.arange(32)[None, :], 8, axis=0)
    return np.tile(one, (1, FRACS)).astype(ml_dtypes.bfloat16)


def dot(a, b, contract):
    return lax.dot_general(a, b, ((contract[:1], contract[1:]), ((), ())), preferred_element_type=F32)


def weights_kernel(place, groups, filters, weight, mirror, first_rows):
    square = jnp.zeros(filters.shape[1:], F32)
    for f in range(FRACS):
        square = square + filters[groups[f]] * filters[groups[f]]
    mine = filters[groups[place[0]]] / jnp.sqrt(square)
    turn = (lax.broadcasted_iota(jnp.int32, (N, N), 0) + lax.broadcasted_iota(jnp.int32, (N, N), 1)) & (N - 1)
    turn = (turn == 0).astype(F32).astype(BF16)
    high = mine.astype(BF16)
    low = (mine - high.astype(F32)).astype(BF16)
    back = dot(high, turn, (1, 0)) + dot(low, turn, (1, 0))
    weight[...] = mine
    mirror[...] = back
    mirror[0:1, :] = mine[0:1]
    mirror[1:2, :] = back[0:1]
    first_rows[0:1, :] = mine[0:1]
    first_rows[1:2, :] = back[0:1]


def start_copies(pairs, sems):
    copies = [pltpu.make_async_copy(a, b, sems.at[i]) for i, (a, b) in enumerate(pairs)]
    for copy in copies:
        copy.start()
    return copies


def lane_hots(spot):
    return (lax.broadcasted_iota(jnp.int32, (128, spot.shape[1]), 0) == (spot & 127)).astype(F32).astype(BF16)


def own_rows_kernel(pixel_in, offset_in, frames_in, gain_in, sent, filled, tail, pixel, offset, frames, gain, fill_map, extended, sems):
    pairs = ((pixel_in, pixel), (offset_in, offset), (frames_in, frames), (gain_in, gain))
    copies = start_copies(pairs, sems)
    copies[0].wait()
    copies[1].wait()
    spot = pixel[...]
    step = offset[...].astype(F32)
    key = ((spot >> 7) & 31) * ROWS + (spot >> 12)
    lane_hot = lane_hots(spot)
    for part in range(4):
        rows = lax.broadcasted_iota(jnp.int32, (256, spot.shape[1]), 0) + 256 * part
        row_hot = jnp.where(rows == key, step, 0.0).astype(BF16)
        found = dot(row_hot, lane_hot, (1, 1))
        for i in range(8):
            lane = (part * 8 + i) * 128
            fill_map[:, lane : lane + 128] = found[i * ROWS : (i + 1) * ROWS]
    copies[2].wait()
    copies[3].wait()
    zero = jnp.zeros((8, N), F32)
    row = lax.broadcasted_iota(jnp.int32, (8, N), 0)
    for c in range(COLS):
        lanes = slice(c * N, (c + 1) * N)
        corrected = frames[:, lanes].astype(F32) * gain[:, lanes].astype(F32)
        extended[0:8, :] = zero
        extended[8 : 8 + ROWS, :] = corrected
        extended[8 + ROWS : 16 + ROWS, :] = zero
        wanted = fill_map[:, lanes]
        value = corrected
        for step in range(-RIM, RIM + 1):
            if step != 0:
                value = jnp.where(wanted == step, extended[8 + step : 8 + step + ROWS, :], value)
        first = jnp.where(row.astype(F32) + wanted[0:8] < 0.0, MARK + wanted[0:8], value[0:8])
        late = jnp.where(row.astype(F32) + wanted[ROWS - 8 :] > 7.0, wanted[ROWS - 8 :], 0.0)
        extended[0:4, :] = corrected[0:4]
        extended[4:8, :] = first[0:4]
        extended[8 : 8 + ROWS, :] = value
        extended[8 + ROWS : 16 + ROWS, :] = late
        sent[:, lanes] = extended[0:8, :].astype(BF16)
        late = jnp.where(row < 4, extended[12 + ROWS : 20 + ROWS, :], 0.0)
        tail[:, lanes] = jnp.concatenate([late, corrected[ROWS - 8 :]], axis=0).astype(BF16)
        window = extended[8 + RIM : 8 + RIM + ROWS, :]
        window = jnp.concatenate([window[: ROWS - 8], jnp.where(row < 4, window[ROWS - 8 :], 0.0)], axis=0)
        filled[c * ROWS : (c + 1) * ROWS, :] = window.astype(BF16)


def columns_kernel(following, filled, tail, table, out, extended, operand):
    row = lax.broadcasted_iota(jnp.int32, (8, N), 0)
    for c in range(COLS):
        lanes = slice(c * N, (c + 1) * N)
        given = following[:, lanes].astype(F32)
        ends = tail[:, lanes].astype(F32)
        extended[0:8, :] = ends[8:16]
        extended[8:16, :] = given
        before = filled[c * ROWS + 16 : (c + 1) * ROWS, :].astype(F32)
        marked = (given > 0.5 * MARK) & (row >= 4)
        wanted = jnp.where(marked, given - MARK, ends[0:8])
        value = jnp.where(row < 4, before[8:16], given)
        for step in range(-RIM, RIM + 1):
            if step != 0:
                value = jnp.where(wanted == step, extended[4 + step : 12 + step, :], value)
        operand[c * ROWS : c * ROWS + 16, :] = filled[c * ROWS : c * ROWS + 16, :]
        operand[c * ROWS + 16 : (c + 1) * ROWS, :] = jnp.concatenate([before[0:8], value], axis=0).astype(BF16)
    out[...] = dot(table[...], operand[...], (1, 1)).astype(BF16)


def rows_kernel(place, spectrum, weight, mirror, following, table, out, by_row, pair):
    tile = place[1]
    lower = tile < HALF
    last = tile == HALF - 1
    for k in range(4):
        if k < 3:
            own = weight[k + 1 : k + 2]
            other = mirror[7 - k : 8 - k]
        else:
            own = jnp.where(lower, following[0:1], weight[4:5])
            other = jnp.where(lower, mirror[1:2], mirror[4:5])
        both = 0.5 * (own + other)
        if k == 3:
            pair[3:4, :] = jnp.where(last, 0.5 * (mirror[0:1] + mirror[1:2]), both)
            both = jnp.where(last, 0.5 * (following[0:1] + following[1:2]), both)
        else:
            pair[k : k + 1, :] = both
        pair[4 + k : 5 + k, :] = both

    group = lax.broadcasted_iota(jnp.int32, (16, 8, 128), 2) >> 5
    wraps = lax.broadcasted_iota(jnp.int32, (8, 128), 1) >= 128 - RIM
    source = spectrum[...].astype(F32).reshape(4, 4, 4, 8, 2 * 128)
    for half in range(2):
        pieces = []
        for j in range(4):
            piece = source[:, :, j, :, half * 128 : (half + 1) * 128].reshape(128, 128)
            pieces.append([piece if d == 0 else pltpu.roll(piece, 32 * d, 1) for d in range(4)])
        for c in range(4):
            found = pieces[3][(3 - c) % 4].reshape(16, 8, 128)
            for j in range(3):
                found = jnp.where(group == j, pieces[j][(j - c) % 4].reshape(16, 8, 128), found)
            for a in range(4):
                for quarter in range(3):
                    by_row[a * 8 + half * 4 + c, :, quarter * 128 : (quarter + 1) * 128] = found[a * 4 + quarter]
                by_row[a * 8 + half * 4 + c, :, 384:] = jnp.where(wraps, found[(a - 1) % 4 * 4 + 3], found[a * 4 + 3])
    operand = by_row[...].reshape(256, N).astype(BF16)
    scale = pair[...][None]
    with_cosine = dot(operand, table[:, :N], (1, 0)).reshape(32, 8, N) * scale
    with_sine = dot(operand, table[:, N:], (1, 0)).reshape(32, 8, N) * scale
    sign = jnp.where(lax.broadcasted_iota(jnp.int32, (1, 8, 1), 1) < 4, 1.0, -1.0)
    total = with_cosine + sign * pltpu.roll(with_sine, 4, 1)
    out[...] = total.reshape(256, N).astype(BF16)


def back_rows_kernel(parts, spread, table, out, both):
    owned = dot(spread[...], parts[...], (1, 0)).astype(BF16)
    turned = dot(table[...], owned, (1, 1))
    real = turned[:N, :128] - turned[N:, 128:]
    imag = turned[:N, 128:] + turned[N:, :128]
    row = lax.broadcasted_iota(jnp.int32, (TILES, 128), 1) & 7
    for part, value in enumerate((real, imag)):
        picked = value[:TILES]
        for y in range(1, 8):
            picked = jnp.where(row == y, value[y * TILES : (y + 1) * TILES], picked)
        both[pl.ds(part, TILES, stride=2), :] = picked * (1.0 / N)
    out[...] = both[...].astype(BF16)


def back_columns_kernel(spectrum, table, out):
    turned = spectrum[...].astype(F32).T.astype(BF16)
    image = dot(turned[:32], table[0], (1, 0))
    for k in range(1, 4):
        image = image + dot(turned[32 * k : 32 * (k + 1)], table[k], (1, 0))
    out[...] = image.reshape(4, 8, N)


def call(kernel, outs, scratch, scalars, cost, *args, vmem=None, limit=VMEM_LIMIT):
    scalar = pl.BlockSpec(memory_space=pltpu.SMEM)
    block = pl.BlockSpec(memory_space=pltpu.VMEM)
    rest = len(args) - scalars
    blocks = rest if vmem is None else vmem
    many = isinstance(outs, (list, tuple))
    return pl.pallas_call(
        kernel,
        out_shape=outs,
        in_specs=[scalar] * scalars + [block] * blocks + [pl.BlockSpec(memory_space=pl.ANY)] * (rest - blocks),
        out_specs=[block] * len(outs) if many else block,
        scratch_shapes=scratch,
        compiler_params=pltpu.CompilerParams(vmem_limit_bytes=limit),
        cost_estimate=pl.CostEstimate(flops=cost, bytes_accessed=1 << 21, transcendentals=0),
    )(*args)


def per_device(frames, gain, defect_pixel, defect_offset, fraction_group, exposure_filter):
    frames = frames.reshape(ROWS, WIDTH)
    place = jnp.stack([lax.axis_index("frac"), lax.axis_index("tile")]).astype(jnp.int32)

    shape = jax.ShapeDtypeStruct
    defects = defect_pixel.shape[0]
    block = (defect_pixel.reshape(1, -1), defect_offset.reshape(1, -1), frames, gain)
    sent, filled, tail = call(
        own_rows_kernel,
        [pltpu.VMEM((8, WIDTH), BF16), pltpu.VMEM((COLS * ROWS, N), BF16), pltpu.VMEM((16, WIDTH), BF16)],
        [
            pltpu.VMEM((1, defects), jnp.int32),
            pltpu.VMEM((1, defects), jnp.int32),
            pltpu.VMEM((ROWS, WIDTH), BF16),
            pltpu.VMEM((ROWS, WIDTH), BF16),
            pltpu.VMEM((ROWS, WIDTH), F32),
            pltpu.VMEM((ROWS + 24, N), F32),
            pltpu.SemaphoreType.DMA((4,)),
        ],
        0,
        1 << 27,
        *(pltpu.with_memory_space_constraint(x, pltpu.HBM) for x in block),
        vmem=0,
        limit=None,
    )
    following_rows = lax.ppermute(sent, "tile", [((t + 1) % TILES, t) for t in range(TILES)])
    weight, mirror, first_rows = call(
        weights_kernel,
        [shape((8, N), F32), shape((8, N), F32), shape((2, N), F32)],
        [],
        2,
        1 << 23,
        place,
        fraction_group,
        exposure_filter,
    )
    mirror = lax.ppermute(mirror, "tile", [(t, TILES - 1 - t) for t in range(TILES)])
    following = lax.ppermute(first_rows, "tile", [((t + 1) % HALF, t) for t in range(HALF)])

    columns = call(
        columns_kernel,
        shape((N, COLS * ROWS), BF16),
        [pltpu.VMEM((16, N), F32), pltpu.VMEM((COLS * ROWS, N), BF16)],
        0,
        1 << 27,
        following_rows,
        filled,
        tail,
        jnp.asarray(forward_columns_table()),
    )
    columns = lax.all_to_all(columns.reshape(TILES, 8, COLS * ROWS), "tile", 0, 0, tiled=True)

    weighted = call(
        rows_kernel,
        shape((256, N), BF16),
        [pltpu.VMEM((32, 8, N), F32), pltpu.VMEM((8, N), F32)],
        1,
        1 << 28,
        place,
        columns.reshape(N, COLS * ROWS),
        weight,
        mirror,
        following,
        jnp.asarray(forward_rows_table()),
    )
    parts = lax.all_to_all(weighted.reshape(FRACS, 32, N), "frac", 0, 0, tiled=True)

    back = call(
        back_rows_kernel,
        shape((2 * TILES, 128), BF16),
        [pltpu.VMEM((2 * TILES, 128), F32)],
        0,
        1 << 28,
        parts.reshape(256, N),
        jnp.asarray(sum_and_spread_table()),
        jnp.asarray(inverse_rows_table()),
    )
    back = lax.all_to_all(back.reshape(TILES, 2, 128), "tile", 0, 0, tiled=True)

    return call(
        back_columns_kernel,
        shape((4, 8, N), F32),
        [],
        0,
        1 << 26,
        back.reshape(2 * TILES, 128),
        jnp.asarray(inverse_columns_table()),
    )


def solution(mesh):
    return jax.shard_map(
        per_device,
        mesh=mesh,
        in_specs=(
            P("frac", "tile", None),
            P("tile", None),
            P("tile"),
            P("tile"),
            P(),
            P(None, "tile", None),
        ),
        out_specs=P("frac", "tile", None),
        check_vma=False,
    )
```

```python
import jax
import jax.numpy as jnp
import ml_dtypes
import numpy as np
from jax import lax
from jax.experimental import pallas as pl
from jax.experimental.pallas import tpu as pltpu
from jax.sharding import PartitionSpec as P

N = 512
RIM = 4
MARK = 64.0
TILES = 64
HALF = TILES // 2
FRACS = 8
COLS = 8
ROWS = 32
WIDTH = N * COLS
F32 = jnp.float32
BF16 = jnp.bfloat16
VMEM_LIMIT = 48 * 1024 * 1024


def wave(a, b):
    angle = (2.0 * np.pi / N) * (np.multiply.outer(a, b) % N)
    return np.cos(angle), np.sin(angle)


def owned_columns():
    tile = np.arange(TILES)[:, None]
    near = np.array([1, 2, 3, 4])[None, :]
    return 8 * tile + np.where(tile < HALF, np.array([1, 2, 3, 8])[None, :], near)


def forward_columns_table():
    cosine, sine = wave(owned_columns(), np.arange(N))
    table = np.stack([cosine, -sine], axis=1)
    table[HALF - 1, 1, 3] = 1.0
    return table.reshape(N, N).astype(ml_dtypes.bfloat16)


def forward_rows_table():
    cosine, sine = wave((np.arange(N) + RIM) % N, np.arange(N))
    return np.concatenate([cosine, sine], axis=1).astype(ml_dtypes.bfloat16)


def inverse_rows_table():
    rows = (8 * np.arange(TILES)[None, :] + np.arange(8)[:, None]).reshape(-1)
    cosine, sine = wave(rows, np.arange(N))
    return np.concatenate([cosine, sine], axis=0).astype(ml_dtypes.bfloat16)


def inverse_columns_table():
    cosine, sine = wave(owned_columns(), np.arange(N))
    table = np.stack([2.0 * cosine, -2.0 * sine], axis=1)
    table[HALF - 1, 0, 3] = 1.0 - 2.0 * (np.arange(N) % 2)
    table[HALF - 1, 1, 3] = 1.0
    table = table.transpose(2, 0, 1, 3) / N
    return table.reshape(4, 2 * TILES, N).astype(ml_dtypes.bfloat16)


def sum_and_spread_table():
    part, k, patch = np.meshgrid(np.arange(2), np.arange(4), np.arange(4), indexing="ij")
    source = (patch * 8 + part * 4 + k).reshape(-1)
    one = np.repeat(source[:, None] == np.arange(32)[None, :], 8, axis=0)
    return np.tile(one, (1, FRACS)).astype(ml_dtypes.bfloat16)


def dot(a, b, contract):
    return lax.dot_general(a, b, ((contract[:1], contract[1:]), ((), ())), preferred_element_type=F32)


def start_copies(pairs, sems):
    copies = [pltpu.make_async_copy(a, b, sems.at[i]) for i, (a, b) in enumerate(pairs)]
    for copy in copies:
        copy.start()
    return copies


def sent_rows_kernel(pixel_in, offset_in, frames_in, gain_in, sent, fill_map, pixel, offset, frames, gain, extended, sems):
    pairs = ((pixel_in, pixel), (offset_in, offset), (frames_in.at[0:16], frames), (gain_in.at[0:16], gain))
    copies = start_copies(pairs, sems)
    copies[0].wait()
    copies[1].wait()
    spot = pixel[...]
    step = offset[...].astype(F32)
    key = ((spot >> 7) & 31) * ROWS + (spot >> 12)
    lane_hot = (lax.broadcasted_iota(jnp.int32, (128, spot.shape[1]), 0) == (spot & 127)).astype(F32).astype(BF16)
    for part in range(4):
        rows = lax.broadcasted_iota(jnp.int32, (256, spot.shape[1]), 0) + 256 * part
        row_hot = jnp.where(rows == key, step, 0.0).astype(BF16)
        found = dot(row_hot, lane_hot, (1, 1)).astype(BF16)
        for i in range(8):
            lane = (part * 8 + i) * 128
            fill_map[:, lane : lane + 128] = found[i * ROWS : (i + 1) * ROWS]
    copies[2].wait()
    copies[3].wait()
    zero = jnp.zeros((8, N), F32)
    row = lax.broadcasted_iota(jnp.int32, (8, N), 0).astype(F32)
    for c in range(COLS):
        lanes = slice(c * N, (c + 1) * N)
        corrected = (frames[:, lanes].astype(F32) * gain[:, lanes].astype(F32))[0:8]
        extended[0:8, :] = zero
        extended[8:16, :] = corrected
        extended[16:24, :] = zero
        wanted = fill_map[0:16, lanes].astype(F32)[0:8]
        value = corrected
        for step in range(-RIM, RIM + 1):
            if step != 0:
                value = jnp.where(wanted == step, extended[8 + step : 16 + step, :], value)
        value = jnp.where(row + wanted < 0.0, MARK + wanted, value)
        extended[0:4, :] = corrected[0:4]
        extended[4:8, :] = value[0:4]
        sent[:, lanes] = extended[0:8, :].astype(BF16)


def own_rows_kernel(fill_map, groups_in, filters_in, frames_in, gain_in, filled, tail, weight, mirror, first_rows, groups, filters, frames, gain, extended, sems):
    pairs = ((groups_in, groups), (filters_in, filters), (frames_in, frames), (gain_in, gain))
    copies = start_copies(pairs, sems)
    turn = (lax.broadcasted_iota(jnp.int32, (N, N), 0) + lax.broadcasted_iota(jnp.int32, (N, N), 1)) & (N - 1)
    turn = (turn == 0).astype(F32).astype(BF16)
    copies[0].wait()
    copies[1].wait()
    square = jnp.zeros(filters.shape[1:], F32)
    for f in range(FRACS):
        square = square + filters[groups[f]] * filters[groups[f]]
    mine = filters[groups[lax.axis_index("frac")]] / jnp.sqrt(square)
    high = mine.astype(BF16)
    low = (mine - high.astype(F32)).astype(BF16)
    back = dot(high, turn, (1, 0)) + dot(low, turn, (1, 0))
    weight[...] = mine
    mirror[...] = back
    mirror[0:1, :] = mine[0:1]
    mirror[1:2, :] = back[0:1]
    first_rows[0:1, :] = mine[0:1]
    first_rows[1:2, :] = back[0:1]

    copies[2].wait()
    copies[3].wait()
    zero = jnp.zeros((8, N), F32)
    row = lax.broadcasted_iota(jnp.int32, (8, N), 0)
    for c in range(COLS):
        lanes = slice(c * N, (c + 1) * N)
        corrected = frames[:, lanes].astype(F32) * gain[:, lanes].astype(F32)
        extended[0:8, :] = zero
        extended[8 : 8 + ROWS, :] = corrected
        extended[8 + ROWS : 16 + ROWS, :] = zero
        wanted = fill_map[:, lanes].astype(F32)
        value = corrected
        for step in range(-RIM, RIM + 1):
            if step != 0:
                value = jnp.where(wanted == step, extended[8 + step : 8 + step + ROWS, :], value)
        late = jnp.where(row.astype(F32) + wanted[ROWS - 8 :] > 7.0, wanted[ROWS - 8 :], 0.0)
        extended[8 : 8 + ROWS, :] = value
        extended[8 + ROWS : 16 + ROWS, :] = late
        late = jnp.where(row < 4, extended[12 + ROWS : 20 + ROWS, :], 0.0)
        tail[:, lanes] = jnp.concatenate([late, corrected[ROWS - 8 :]], axis=0).astype(BF16)
        window = extended[8 + RIM : 8 + RIM + ROWS, :]
        window = jnp.concatenate([window[: ROWS - 8], jnp.where(row < 4, window[ROWS - 8 :], 0.0)], axis=0)
        filled[c * ROWS : (c + 1) * ROWS, :] = window.astype(BF16)


def columns_kernel(following, filled, tail, table, out, extended, operand):
    row = lax.broadcasted_iota(jnp.int32, (8, N), 0)
    for c in range(COLS):
        lanes = slice(c * N, (c + 1) * N)
        given = following[:, lanes].astype(F32)
        ends = tail[:, lanes].astype(F32)
        extended[0:8, :] = ends[8:16]
        extended[8:16, :] = given
        before = filled[c * ROWS + 16 : (c + 1) * ROWS, :].astype(F32)
        marked = (given > 0.5 * MARK) & (row >= 4)
        wanted = jnp.where(marked, given - MARK, ends[0:8])
        value = jnp.where(row < 4, before[8:16], given)
        for step in range(-RIM, RIM + 1):
            if step != 0:
                value = jnp.where(wanted == step, extended[4 + step : 12 + step, :], value)
        operand[c * ROWS : c * ROWS + 16, :] = filled[c * ROWS : c * ROWS + 16, :]
        operand[c * ROWS + 16 : (c + 1) * ROWS, :] = jnp.concatenate([before[0:8], value], axis=0).astype(BF16)
    out[...] = dot(table[...], operand[...], (1, 1)).astype(BF16)


def rows_kernel(spectrum, weight, mirror, following, table, out, by_row, pair):
    tile = lax.axis_index("tile")
    lower = tile < HALF
    last = tile == HALF - 1
    for k in range(4):
        if k < 3:
            own = weight[k + 1 : k + 2]
            other = mirror[7 - k : 8 - k]
        else:
            own = jnp.where(lower, following[0:1], weight[4:5])
            other = jnp.where(lower, mirror[1:2], mirror[4:5])
        both = 0.5 * (own + other)
        if k == 3:
            pair[3:4, :] = jnp.where(last, 0.5 * (mirror[0:1] + mirror[1:2]), both)
            both = jnp.where(last, 0.5 * (following[0:1] + following[1:2]), both)
        else:
            pair[k : k + 1, :] = both
        pair[4 + k : 5 + k, :] = both

    group = lax.broadcasted_iota(jnp.int32, (16, 8, 128), 2) >> 5
    wraps = lax.broadcasted_iota(jnp.int32, (8, 128), 1) >= 128 - RIM
    source = spectrum[...].astype(F32).reshape(4, 4, 4, 8, 2 * 128)
    for half in range(2):
        pieces = []
        for j in range(4):
            piece = source[:, :, j, :, half * 128 : (half + 1) * 128].reshape(128, 128)
            pieces.append([piece if d == 0 else pltpu.roll(piece, 32 * d, 1) for d in range(4)])
        for c in range(4):
            found = pieces[3][(3 - c) % 4].reshape(16, 8, 128)
            for j in range(3):
                found = jnp.where(group == j, pieces[j][(j - c) % 4].reshape(16, 8, 128), found)
            for a in range(4):
                for quarter in range(3):
                    by_row[a * 8 + half * 4 + c, :, quarter * 128 : (quarter + 1) * 128] = found[a * 4 + quarter]
                by_row[a * 8 + half * 4 + c, :, 384:] = jnp.where(wraps, found[(a - 1) % 4 * 4 + 3], found[a * 4 + 3])
    operand = by_row[...].reshape(256, N).astype(BF16)
    scale = pair[...][None]
    with_cosine = dot(operand, table[:, :N], (1, 0)).reshape(32, 8, N) * scale
    with_sine = dot(operand, table[:, N:], (1, 0)).reshape(32, 8, N) * scale
    sign = jnp.where(lax.broadcasted_iota(jnp.int32, (1, 8, 1), 1) < 4, 1.0, -1.0)
    total = with_cosine + sign * pltpu.roll(with_sine, 4, 1)
    out[...] = total.reshape(256, N).astype(BF16)


def back_rows_kernel(parts, spread, table, out, both):
    owned = dot(spread[...], parts[...], (1, 0)).astype(BF16)
    turned = dot(table[...], owned, (1, 1))
    real = turned[:N, :128] - turned[N:, 128:]
    imag = turned[:N, 128:] + turned[N:, :128]
    row = lax.broadcasted_iota(jnp.int32, (TILES, 128), 1) & 7
    for part, value in enumerate((real, imag)):
        picked = value[:TILES]
        for y in range(1, 8):
            picked = jnp.where(row == y, value[y * TILES : (y + 1) * TILES], picked)
        both[pl.ds(part, TILES, stride=2), :] = picked * (1.0 / N)
    out[...] = both[...].astype(BF16)


def back_columns_kernel(spectrum, table, out):
    turned = spectrum[...].astype(F32).T.astype(BF16)
    image = dot(turned[:32], table[0], (1, 0))
    for k in range(1, 4):
        image = image + dot(turned[32 * k : 32 * (k + 1)], table[k], (1, 0))
    out[...] = image.reshape(4, 8, N)


def call(kernel, outs, scratch, cost, *args, vmem=None):
    block = pl.BlockSpec(memory_space=pltpu.VMEM)
    blocks = len(args) if vmem is None else vmem
    many = isinstance(outs, (list, tuple))
    return pl.pallas_call(
        kernel,
        out_shape=outs,
        in_specs=[block] * blocks + [pl.BlockSpec(memory_space=pl.ANY)] * (len(args) - blocks),
        out_specs=[block] * len(outs) if many else block,
        scratch_shapes=scratch,
        compiler_params=pltpu.CompilerParams(vmem_limit_bytes=VMEM_LIMIT),
        cost_estimate=pl.CostEstimate(flops=cost, bytes_accessed=1 << 21, transcendentals=0),
    )(*args)


def per_device(frames, gain, defect_pixel, defect_offset, fraction_group, exposure_filter):
    frames = frames.reshape(ROWS, WIDTH)

    shape = jax.ShapeDtypeStruct
    defects = defect_pixel.shape[0]
    def stay(x):
        return pltpu.with_memory_space_constraint(x, pltpu.HBM)

    frames, gain = stay(frames), stay(gain)
    sent, fill_map = call(
        sent_rows_kernel,
        [pltpu.VMEM((8, WIDTH), BF16), pltpu.VMEM((ROWS, WIDTH), BF16)],
        [
            pltpu.VMEM((1, defects), jnp.int32),
            pltpu.VMEM((1, defects), jnp.int32),
            pltpu.VMEM((16, WIDTH), BF16),
            pltpu.VMEM((16, WIDTH), BF16),
            pltpu.VMEM((24, N), F32),
            pltpu.SemaphoreType.DMA((4,)),
        ],
        1 << 27,
        stay(defect_pixel.reshape(1, -1)),
        stay(defect_offset.reshape(1, -1)),
        frames,
        gain,
        vmem=0,
    )
    following_rows = lax.ppermute(sent, "tile", [((t + 1) % TILES, t) for t in range(TILES)])
    filled, tail, weight, mirror, first_rows = call(
        own_rows_kernel,
        [
            pltpu.VMEM((COLS * ROWS, N), BF16),
            pltpu.VMEM((16, WIDTH), BF16),
            pltpu.VMEM((8, N), F32),
            pltpu.VMEM((8, N), F32),
            pltpu.VMEM((2, N), F32),
        ],
        [
            pltpu.SMEM((FRACS,), jnp.int32),
            pltpu.VMEM((8, 8, N), F32),
            pltpu.VMEM((ROWS, WIDTH), BF16),
            pltpu.VMEM((ROWS, WIDTH), BF16),
            pltpu.VMEM((ROWS + 24, N), F32),
            pltpu.SemaphoreType.DMA((4,)),
        ],
        1 << 27,
        fill_map,
        stay(fraction_group),
        stay(exposure_filter),
        frames,
        gain,
        vmem=1,
    )
    mirror = lax.ppermute(mirror, "tile", [(t, TILES - 1 - t) for t in range(TILES)])
    following = lax.ppermute(first_rows, "tile", [((t + 1) % HALF, t) for t in range(HALF)])

    columns = call(
        columns_kernel,
        shape((N, COLS * ROWS), BF16),
        [pltpu.VMEM((16, N), F32), pltpu.VMEM((COLS * ROWS, N), BF16)],
        1 << 27,
        following_rows,
        filled,
        tail,
        jnp.asarray(forward_columns_table()),
    )
    columns = lax.all_to_all(columns.reshape(TILES, 8, COLS * ROWS), "tile", 0, 0, tiled=True)

    weighted = call(
        rows_kernel,
        shape((256, N), BF16),
        [pltpu.VMEM((32, 8, N), F32), pltpu.VMEM((8, N), F32)],
        1 << 28,
        columns.reshape(N, COLS * ROWS),
        weight,
        mirror,
        following,
        jnp.asarray(forward_rows_table()),
    )
    parts = lax.all_to_all(weighted.reshape(FRACS, 32, N), "frac", 0, 0, tiled=True)

    back = call(
        back_rows_kernel,
        shape((2 * TILES, 128), BF16),
        [pltpu.VMEM((2 * TILES, 128), F32)],
        1 << 28,
        parts.reshape(256, N),
        jnp.asarray(sum_and_spread_table()),
        jnp.asarray(inverse_rows_table()),
    )
    back = lax.all_to_all(back.reshape(TILES, 2, 128), "tile", 0, 0, tiled=True)

    return call(
        back_columns_kernel,
        shape((4, 8, N), F32),
        [],
        1 << 26,
        back.reshape(2 * TILES, 128),
        jnp.asarray(inverse_columns_table()),
    )


def solution(mesh):
    return jax.shard_map(
        per_device,
        mesh=mesh,
        in_specs=(
            P("frac", "tile", None),
            P("tile", None),
            P("tile"),
            P("tile"),
            P(),
            P(None, "tile", None),
        ),
        out_specs=P("frac", "tile", None),
        check_vma=False,
    )
```

```python
import jax
import jax.numpy as jnp
import ml_dtypes
import numpy as np
from jax import lax
from jax.experimental import pallas as pl
from jax.experimental.pallas import tpu as pltpu
from jax.sharding import PartitionSpec as P

N = 512
RIM = 4
MARK = 64.0
TILES = 64
HALF = TILES // 2
FIRST_ORDER = [(i + 60) % TILES for i in range(TILES)]
FRACTION_ORDER = [(i + 5) % 8 for i in range(8)]
LAST_ORDER = [(i + 40) % TILES for i in range(TILES)]
FRACS = 8
COLS = 8
ROWS = 32
WIDTH = N * COLS
F32 = jnp.float32
BF16 = jnp.bfloat16
VMEM_LIMIT = 48 * 1024 * 1024


def wave(a, b):
    angle = (2.0 * np.pi / N) * (np.multiply.outer(a, b) % N)
    return np.cos(angle), np.sin(angle)


def owned_columns():
    tile = np.arange(TILES)[:, None]
    near = np.array([1, 2, 3, 4])[None, :]
    return 8 * tile + np.where(tile < HALF, np.array([1, 2, 3, 8])[None, :], near)


def forward_columns_table():
    cosine, sine = wave(owned_columns(), np.arange(N))
    table = np.stack([cosine, -sine], axis=1)
    table[HALF - 1, 1, 3] = 1.0
    table = table[FIRST_ORDER]
    return table.reshape(N, N).astype(ml_dtypes.bfloat16)


def forward_rows_table():
    cosine, sine = wave((np.arange(N) + RIM) % N, np.arange(N))
    return np.concatenate([cosine, sine], axis=1).astype(ml_dtypes.bfloat16)


def inverse_rows_table():
    rows = (8 * np.array(LAST_ORDER)[None, :] + np.arange(8)[:, None]).reshape(-1)
    cosine, sine = wave(rows, np.arange(N))
    return np.concatenate([cosine, sine], axis=0).astype(ml_dtypes.bfloat16)


def inverse_columns_table():
    cosine, sine = wave(owned_columns(), np.arange(N))
    table = np.stack([2.0 * cosine, -2.0 * sine], axis=1)
    table[HALF - 1, 0, 3] = 1.0 - 2.0 * (np.arange(N) % 2)
    table[HALF - 1, 1, 3] = 1.0
    table = table[LAST_ORDER].transpose(2, 0, 1, 3) / N
    return table.reshape(4, 2 * TILES, N).astype(ml_dtypes.bfloat16)


def sum_and_spread_table():
    part, k, patch = np.meshgrid(np.arange(2), np.arange(4), np.arange(4), indexing="ij")
    source = (patch * 8 + part * 4 + k).reshape(-1)
    one = np.repeat(source[:, None] == np.arange(32)[None, :], 8, axis=0)
    return np.tile(one, (1, FRACS)).astype(ml_dtypes.bfloat16)


def dot(a, b, contract):
    return lax.dot_general(a, b, ((contract[:1], contract[1:]), ((), ())), preferred_element_type=F32)


def start_copies(pairs, sems):
    copies = [pltpu.make_async_copy(a, b, sems.at[i]) for i, (a, b) in enumerate(pairs)]
    for copy in copies:
        copy.start()
    return copies


def sent_rows_kernel(pixel_in, offset_in, frames_in, gain_in, sent, fill_map, pixel, offset, frames, gain, extended, sems):
    pairs = ((pixel_in, pixel), (offset_in, offset), (frames_in.at[0:16], frames), (gain_in.at[0:16], gain))
    copies = start_copies(pairs, sems)
    copies[0].wait()
    copies[1].wait()
    spot = pixel[...]
    step = offset[...].astype(F32)
    key = ((spot >> 7) & 31) * ROWS + (spot >> 12)
    lane_hot = (lax.broadcasted_iota(jnp.int32, (128, spot.shape[1]), 0) == (spot & 127)).astype(F32).astype(BF16)
    for part in range(4):
        rows = lax.broadcasted_iota(jnp.int32, (256, spot.shape[1]), 0) + 256 * part
        row_hot = jnp.where(rows == key, step, 0.0).astype(BF16)
        found = dot(row_hot, lane_hot, (1, 1)).astype(BF16)
        for i in range(8):
            lane = (part * 8 + i) * 128
            fill_map[:, lane : lane + 128] = found[i * ROWS : (i + 1) * ROWS]
    copies[2].wait()
    copies[3].wait()
    zero = jnp.zeros((8, N), F32)
    row = lax.broadcasted_iota(jnp.int32, (8, N), 0).astype(F32)
    for c in range(COLS):
        lanes = slice(c * N, (c + 1) * N)
        corrected = (frames[:, lanes].astype(F32) * gain[:, lanes].astype(F32))[0:8]
        extended[0:8, :] = zero
        extended[8:16, :] = corrected
        extended[16:24, :] = zero
        wanted = fill_map[0:16, lanes].astype(F32)[0:8]
        value = corrected
        for step in range(-RIM, RIM + 1):
            if step != 0:
                value = jnp.where(wanted == step, extended[8 + step : 16 + step, :], value)
        value = jnp.where(row + wanted < 0.0, MARK + wanted, value)
        extended[0:4, :] = corrected[0:4]
        extended[4:8, :] = value[0:4]
        sent[:, lanes] = extended[0:8, :].astype(BF16)


def own_rows_kernel(fill_map, groups_in, filters_in, frames_in, gain_in, filled, tail, weight, mirror, first_rows, groups, filters, frames, gain, extended, sems):
    pairs = ((groups_in, groups), (filters_in, filters), (frames_in, frames), (gain_in, gain))
    copies = start_copies(pairs, sems)
    turn = (lax.broadcasted_iota(jnp.int32, (N, N), 0) + lax.broadcasted_iota(jnp.int32, (N, N), 1)) & (N - 1)
    turn = (turn == 0).astype(F32).astype(BF16)
    copies[0].wait()
    copies[1].wait()
    square = jnp.zeros(filters.shape[1:], F32)
    for f in range(FRACS):
        square = square + filters[groups[f]] * filters[groups[f]]
    mine = filters[groups[lax.axis_index("frac")]] / jnp.sqrt(square)
    high = mine.astype(BF16)
    low = (mine - high.astype(F32)).astype(BF16)
    back = dot(high, turn, (1, 0)) + dot(low, turn, (1, 0))
    weight[...] = mine
    mirror[...] = back
    mirror[0:1, :] = mine[0:1]
    mirror[1:2, :] = back[0:1]
    first_rows[0:1, :] = mine[0:1]
    first_rows[1:2, :] = back[0:1]

    copies[2].wait()
    copies[3].wait()
    zero = jnp.zeros((8, N), F32)
    row = lax.broadcasted_iota(jnp.int32, (8, N), 0)
    for c in range(COLS):
        lanes = slice(c * N, (c + 1) * N)
        corrected = frames[:, lanes].astype(F32) * gain[:, lanes].astype(F32)
        extended[0:8, :] = zero
        extended[8 : 8 + ROWS, :] = corrected
        extended[8 + ROWS : 16 + ROWS, :] = zero
        wanted = fill_map[:, lanes].astype(F32)
        value = corrected
        for step in range(-RIM, RIM + 1):
            if step != 0:
                value = jnp.where(wanted == step, extended[8 + step : 8 + step + ROWS, :], value)
        late = jnp.where(row.astype(F32) + wanted[ROWS - 8 :] > 7.0, wanted[ROWS - 8 :], 0.0)
        extended[8 : 8 + ROWS, :] = value
        extended[8 + ROWS : 16 + ROWS, :] = late
        late = jnp.where(row < 4, extended[12 + ROWS : 20 + ROWS, :], 0.0)
        tail[:, lanes] = jnp.concatenate([late, corrected[ROWS - 8 :]], axis=0).astype(BF16)
        window = extended[8 + RIM : 8 + RIM + ROWS, :]
        window = jnp.concatenate([window[: ROWS - 8], jnp.where(row < 4, window[ROWS - 8 :], 0.0)], axis=0)
        filled[c * ROWS : (c + 1) * ROWS, :] = window.astype(BF16)


def columns_kernel(following, filled, tail, table, out, extended, operand):
    row = lax.broadcasted_iota(jnp.int32, (8, N), 0)
    for c in range(COLS):
        lanes = slice(c * N, (c + 1) * N)
        given = following[:, lanes].astype(F32)
        ends = tail[:, lanes].astype(F32)
        extended[0:8, :] = ends[8:16]
        extended[8:16, :] = given
        before = filled[c * ROWS + 16 : (c + 1) * ROWS, :].astype(F32)
        marked = (given > 0.5 * MARK) & (row >= 4)
        wanted = jnp.where(marked, given - MARK, ends[0:8])
        value = jnp.where(row < 4, before[8:16], given)
        for step in range(-RIM, RIM + 1):
            if step != 0:
                value = jnp.where(wanted == step, extended[4 + step : 12 + step, :], value)
        operand[c * ROWS : c * ROWS + 16, :] = filled[c * ROWS : c * ROWS + 16, :]
        operand[c * ROWS + 16 : (c + 1) * ROWS, :] = jnp.concatenate([before[0:8], value], axis=0).astype(BF16)
    out[...] = dot(table[...], operand[...], (1, 1)).astype(BF16)


def rows_kernel(spectrum, weight, mirror, following, table, out, by_row, pair):
    tile = lax.axis_index("tile")
    lower = tile < HALF
    last = tile == HALF - 1
    for k in range(4):
        if k < 3:
            own = weight[k + 1 : k + 2]
            other = mirror[7 - k : 8 - k]
        else:
            own = jnp.where(lower, following[0:1], weight[4:5])
            other = jnp.where(lower, mirror[1:2], mirror[4:5])
        both = 0.5 * (own + other)
        if k == 3:
            pair[3:4, :] = jnp.where(last, 0.5 * (mirror[0:1] + mirror[1:2]), both)
            both = jnp.where(last, 0.5 * (following[0:1] + following[1:2]), both)
        else:
            pair[k : k + 1, :] = both
        pair[4 + k : 5 + k, :] = both

    group = lax.broadcasted_iota(jnp.int32, (16, 8, 128), 2) >> 5
    wraps = lax.broadcasted_iota(jnp.int32, (8, 128), 1) >= 128 - RIM
    place = [8 * FIRST_ORDER.index(t) for t in range(TILES)]
    source = spectrum[...].astype(F32)
    source = jnp.concatenate([source[place[t] : place[t] + 8] for t in range(TILES)], axis=0)
    source = source.reshape(4, 4, 4, 8, 2 * 128)
    for half in range(2):
        pieces = []
        for j in range(4):
            piece = source[:, :, j, :, half * 128 : (half + 1) * 128].reshape(128, 128)
            pieces.append([piece if d == 0 else pltpu.roll(piece, 32 * d, 1) for d in range(4)])
        for c in range(4):
            found = pieces[3][(3 - c) % 4].reshape(16, 8, 128)
            for j in range(3):
                found = jnp.where(group == j, pieces[j][(j - c) % 4].reshape(16, 8, 128), found)
            for a in range(4):
                row = FRACTION_ORDER.index(2 * a + half) * 4 + c
                for quarter in range(3):
                    by_row[row, :, quarter * 128 : (quarter + 1) * 128] = found[a * 4 + quarter]
                by_row[row, :, 384:] = jnp.where(wraps, found[(a - 1) % 4 * 4 + 3], found[a * 4 + 3])
    operand = by_row[...].reshape(256, N).astype(BF16)
    scale = pair[...][None]
    with_cosine = dot(operand, table[:, :N], (1, 0)).reshape(32, 8, N) * scale
    with_sine = dot(operand, table[:, N:], (1, 0)).reshape(32, 8, N) * scale
    sign = jnp.where(lax.broadcasted_iota(jnp.int32, (1, 8, 1), 1) < 4, 1.0, -1.0)
    total = with_cosine + sign * pltpu.roll(with_sine, 4, 1)
    out[...] = total.reshape(256, N).astype(BF16)


def back_rows_kernel(parts, spread, table, out, both):
    owned = dot(spread[...], parts[...], (1, 0)).astype(BF16)
    turned = dot(table[...], owned, (1, 1))
    real = turned[:N, :128] - turned[N:, 128:]
    imag = turned[:N, 128:] + turned[N:, :128]
    row = lax.broadcasted_iota(jnp.int32, (TILES, 128), 1) & 7
    for part, value in enumerate((real, imag)):
        picked = value[:TILES]
        for y in range(1, 8):
            picked = jnp.where(row == y, value[y * TILES : (y + 1) * TILES], picked)
        both[pl.ds(part, TILES, stride=2), :] = picked * (1.0 / N)
    out[...] = both[...].astype(BF16)


def back_columns_kernel(spectrum, table, out):
    turned = spectrum[...].astype(F32).T.astype(BF16)
    image = dot(turned[:32], table[0], (1, 0))
    for k in range(1, 4):
        image = image + dot(turned[32 * k : 32 * (k + 1)], table[k], (1, 0))
    out[...] = image.reshape(4, 8, N)


def call(kernel, outs, scratch, cost, *args, vmem=None):
    block = pl.BlockSpec(memory_space=pltpu.VMEM)
    blocks = len(args) if vmem is None else vmem
    many = isinstance(outs, (list, tuple))
    return pl.pallas_call(
        kernel,
        out_shape=outs,
        in_specs=[block] * blocks + [pl.BlockSpec(memory_space=pl.ANY)] * (len(args) - blocks),
        out_specs=[block] * len(outs) if many else block,
        scratch_shapes=scratch,
        compiler_params=pltpu.CompilerParams(vmem_limit_bytes=VMEM_LIMIT),
        cost_estimate=pl.CostEstimate(flops=cost, bytes_accessed=1 << 21, transcendentals=0),
    )(*args)


def exchange(blocks, axis, order):
    return lax.all_to_all(blocks, axis, 0, 0, axis_index_groups=[order], tiled=True)


def per_device(frames, gain, defect_pixel, defect_offset, fraction_group, exposure_filter):
    frames = frames.reshape(ROWS, WIDTH)

    shape = jax.ShapeDtypeStruct
    defects = defect_pixel.shape[0]
    def stay(x):
        return pltpu.with_memory_space_constraint(x, pltpu.HBM)

    frames, gain = stay(frames), stay(gain)
    sent, fill_map = call(
        sent_rows_kernel,
        [pltpu.VMEM((8, WIDTH), BF16), pltpu.VMEM((ROWS, WIDTH), BF16)],
        [
            pltpu.VMEM((1, defects), jnp.int32),
            pltpu.VMEM((1, defects), jnp.int32),
            pltpu.VMEM((16, WIDTH), BF16),
            pltpu.VMEM((16, WIDTH), BF16),
            pltpu.VMEM((24, N), F32),
            pltpu.SemaphoreType.DMA((4,)),
        ],
        1 << 27,
        stay(defect_pixel.reshape(1, -1)),
        stay(defect_offset.reshape(1, -1)),
        frames,
        gain,
        vmem=0,
    )
    following_rows = lax.ppermute(sent, "tile", [((t + 1) % TILES, t) for t in range(TILES)])
    filled, tail, weight, mirror, first_rows = call(
        own_rows_kernel,
        [
            pltpu.VMEM((COLS * ROWS, N), BF16),
            pltpu.VMEM((16, WIDTH), BF16),
            pltpu.VMEM((8, N), F32),
            pltpu.VMEM((8, N), F32),
            pltpu.VMEM((2, N), F32),
        ],
        [
            pltpu.SMEM((FRACS,), jnp.int32),
            pltpu.VMEM((8, 8, N), F32),
            pltpu.VMEM((ROWS, WIDTH), BF16),
            pltpu.VMEM((ROWS, WIDTH), BF16),
            pltpu.VMEM((ROWS + 24, N), F32),
            pltpu.SemaphoreType.DMA((4,)),
        ],
        1 << 27,
        fill_map,
        stay(fraction_group),
        stay(exposure_filter),
        frames,
        gain,
        vmem=1,
    )
    mirror = lax.ppermute(mirror, "tile", [(t, TILES - 1 - t) for t in range(TILES)])
    following = lax.ppermute(first_rows, "tile", [((t + 1) % HALF, t) for t in range(HALF)])

    columns = call(
        columns_kernel,
        shape((N, COLS * ROWS), BF16),
        [pltpu.VMEM((16, N), F32), pltpu.VMEM((COLS * ROWS, N), BF16)],
        1 << 27,
        following_rows,
        filled,
        tail,
        jnp.asarray(forward_columns_table()),
    )
    columns = exchange(columns.reshape(TILES, 8, COLS * ROWS), "tile", FIRST_ORDER)

    weighted = call(
        rows_kernel,
        shape((256, N), BF16),
        [pltpu.VMEM((32, 8, N), F32), pltpu.VMEM((8, N), F32)],
        1 << 28,
        columns.reshape(N, COLS * ROWS),
        weight,
        mirror,
        following,
        jnp.asarray(forward_rows_table()),
    )
    parts = exchange(weighted.reshape(FRACS, 32, N), "frac", FRACTION_ORDER)

    back = call(
        back_rows_kernel,
        shape((2 * TILES, 128), BF16),
        [pltpu.VMEM((2 * TILES, 128), F32)],
        1 << 28,
        parts.reshape(256, N),
        jnp.asarray(sum_and_spread_table()),
        jnp.asarray(inverse_rows_table()),
    )
    back = exchange(back.reshape(TILES, 2, 128), "tile", LAST_ORDER)

    return call(
        back_columns_kernel,
        shape((4, 8, N), F32),
        [],
        1 << 26,
        back.reshape(2 * TILES, 128),
        jnp.asarray(inverse_columns_table()),
    )


def solution(mesh):
    return jax.shard_map(
        per_device,
        mesh=mesh,
        in_specs=(
            P("frac", "tile", None),
            P("tile", None),
            P("tile"),
            P("tile"),
            P(),
            P(None, "tile", None),
        ),
        out_specs=P("frac", "tile", None),
        check_vma=False,
    )
```

```python
import jax
import jax.numpy as jnp
import ml_dtypes
import numpy as np
from jax import lax
from jax.experimental import pallas as pl
from jax.experimental.pallas import tpu as pltpu
from jax.sharding import PartitionSpec as P

N = 512
RIM = 4
MARK = 64.0
TILES = 64
HALF = TILES // 2
FIRST_ORDER = [(i + 60) % TILES for i in range(TILES)]
FRACTION_ORDER = [(i + 5) % 8 for i in range(8)]
LAST_ORDER = [(i + 40) % TILES for i in range(TILES)]
FRACS = 8
COLS = 8
ROWS = 32
WIDTH = N * COLS
F32 = jnp.float32
BF16 = jnp.bfloat16
VMEM_LIMIT = 48 * 1024 * 1024


def wave(a, b):
    angle = (2.0 * np.pi / N) * (np.multiply.outer(a, b) % N)
    return np.cos(angle), np.sin(angle)


def owned_columns():
    tile = np.arange(TILES)[:, None]
    near = np.array([1, 2, 3, 4])[None, :]
    return 8 * tile + np.where(tile < HALF, np.array([1, 2, 3, 8])[None, :], near)


def forward_columns_table():
    cosine, sine = wave(owned_columns(), np.arange(N))
    table = np.stack([cosine, -sine], axis=1)
    table[HALF - 1, 1, 3] = 1.0
    table = table[FIRST_ORDER]
    return table.reshape(N, N).astype(ml_dtypes.bfloat16)


def forward_rows_table():
    cosine, sine = wave((np.arange(N) + RIM) % N, np.arange(N))
    return np.concatenate([cosine, sine], axis=1).astype(ml_dtypes.bfloat16)


def inverse_rows_table():
    rows = (8 * np.array(LAST_ORDER)[None, :] + np.arange(8)[:, None]).reshape(-1)
    cosine, sine = wave(rows, np.arange(N))
    return np.concatenate([cosine, sine], axis=0).astype(ml_dtypes.bfloat16)


def inverse_columns_table():
    cosine, sine = wave(owned_columns(), np.arange(N))
    table = np.stack([2.0 * cosine, -2.0 * sine], axis=1)
    table[HALF - 1, 0, 3] = 1.0 - 2.0 * (np.arange(N) % 2)
    table[HALF - 1, 1, 3] = 1.0
    table = table[LAST_ORDER].transpose(2, 0, 1, 3) / N
    return table.reshape(N, N).astype(ml_dtypes.bfloat16)


def sum_and_spread_table():
    part, k, patch = np.meshgrid(np.arange(2), np.arange(4), np.arange(4), indexing="ij")
    source = (patch * 8 + part * 4 + k).reshape(-1)
    one = np.repeat(source[:, None] == np.arange(32)[None, :], 8, axis=0)
    return np.tile(one, (1, FRACS)).astype(ml_dtypes.bfloat16)


def dot(a, b, contract):
    return lax.dot_general(a, b, ((contract[:1], contract[1:]), ((), ())), preferred_element_type=F32)


def start_copies(pairs, sems):
    copies = [pltpu.make_async_copy(a, b, sems.at[i]) for i, (a, b) in enumerate(pairs)]
    for copy in copies:
        copy.start()
    return copies


def sent_rows_kernel(pixel_in, offset_in, frames_in, gain_in, sent, fill_map, pixel, offset, frames, gain, extended, sems):
    pairs = ((pixel_in, pixel), (offset_in, offset), (frames_in.at[0:16], frames), (gain_in.at[0:16], gain))
    copies = start_copies(pairs, sems)
    copies[0].wait()
    copies[1].wait()
    spot = pixel[...]
    step = offset[...].astype(F32)
    key = ((spot >> 7) & 31) * ROWS + (spot >> 12)
    lane_hot = (lax.broadcasted_iota(jnp.int32, (128, spot.shape[1]), 0) == (spot & 127)).astype(F32).astype(BF16)
    for part in range(4):
        rows = lax.broadcasted_iota(jnp.int32, (256, spot.shape[1]), 0) + 256 * part
        row_hot = jnp.where(rows == key, step, 0.0).astype(BF16)
        found = dot(row_hot, lane_hot, (1, 1)).astype(BF16)
        for i in range(8):
            lane = (part * 8 + i) * 128
            fill_map[:, lane : lane + 128] = found[i * ROWS : (i + 1) * ROWS]
    copies[2].wait()
    copies[3].wait()
    extended[0:8, :] = jnp.zeros((8, N), F32)
    extended[16:24, :] = jnp.zeros((8, N), F32)
    row = lax.broadcasted_iota(jnp.int32, (8, N), 0).astype(F32)
    for c in range(COLS):
        lanes = slice(c * N, (c + 1) * N)
        corrected = (frames[:, lanes].astype(F32) * gain[:, lanes].astype(F32))[0:8]
        extended[8:16, :] = corrected
        wanted = fill_map[0:16, lanes].astype(F32)[0:8]
        value = corrected
        for step in range(-RIM, RIM + 1):
            if step != 0:
                value = jnp.where(wanted == step, extended[8 + step : 16 + step, :], value)
        value = jnp.where(row + wanted < 0.0, MARK + wanted, value)
        extended[24:28, :] = corrected[0:4]
        extended[28:32, :] = value[0:4]
        sent[:, lanes] = extended[24:32, :].astype(BF16)


def own_rows_kernel(fill_map, groups_in, filters_in, frames_in, gain_in, filled, tail, weight, mirror, first_rows, groups, filters, frames, gain, extended, sems):
    pairs = ((groups_in, groups), (filters_in, filters), (frames_in, frames), (gain_in, gain))
    copies = start_copies(pairs, sems)
    turn = (lax.broadcasted_iota(jnp.int32, (N, N), 0) + lax.broadcasted_iota(jnp.int32, (N, N), 1)) & (N - 1)
    turn = (turn == 0).astype(F32).astype(BF16)
    copies[0].wait()
    copies[1].wait()
    square = jnp.zeros(filters.shape[1:], F32)
    for f in range(FRACS):
        square = square + filters[groups[f]] * filters[groups[f]]
    mine = filters[groups[lax.axis_index("frac")]] / jnp.sqrt(square)
    high = mine.astype(BF16)
    low = (mine - high.astype(F32)).astype(BF16)
    back = dot(high, turn, (1, 0)) + dot(low, turn, (1, 0))
    weight[...] = mine
    mirror[...] = back
    mirror[0:1, :] = mine[0:1]
    mirror[1:2, :] = back[0:1]
    first_rows[0:1, :] = mine[0:1]
    first_rows[1:2, :] = back[0:1]

    copies[2].wait()
    copies[3].wait()
    zero = jnp.zeros((8, N), F32)
    row = lax.broadcasted_iota(jnp.int32, (8, N), 0)
    for c in range(COLS):
        lanes = slice(c * N, (c + 1) * N)
        corrected = frames[:, lanes].astype(F32) * gain[:, lanes].astype(F32)
        extended[0:8, :] = zero
        extended[8 : 8 + ROWS, :] = corrected
        extended[8 + ROWS : 16 + ROWS, :] = zero
        wanted = fill_map[:, lanes].astype(F32)
        value = corrected
        for step in range(-RIM, RIM + 1):
            if step != 0:
                value = jnp.where(wanted == step, extended[8 + step : 8 + step + ROWS, :], value)
        late = jnp.where(row.astype(F32) + wanted[ROWS - 8 :] > 7.0, wanted[ROWS - 8 :], 0.0)
        extended[8 : 8 + ROWS, :] = value
        extended[8 + ROWS : 16 + ROWS, :] = late
        late = jnp.where(row < 4, extended[12 + ROWS : 20 + ROWS, :], 0.0)
        tail[:, lanes] = jnp.concatenate([late, corrected[ROWS - 8 :]], axis=0).astype(BF16)
        window = extended[8 + RIM : 8 + RIM + ROWS, :]
        window = jnp.concatenate([window[: ROWS - 8], jnp.where(row < 4, window[ROWS - 8 :], 0.0)], axis=0)
        filled[c * ROWS : (c + 1) * ROWS, :] = window.astype(BF16)


def columns_kernel(following, filled, tail, table, out, extended, operand):
    row = lax.broadcasted_iota(jnp.int32, (8, N), 0)
    for c in range(COLS):
        lanes = slice(c * N, (c + 1) * N)
        given = following[:, lanes].astype(F32)
        ends = tail[:, lanes].astype(F32)
        extended[0:8, :] = ends[8:16]
        extended[8:16, :] = given
        before = filled[c * ROWS + 16 : (c + 1) * ROWS, :].astype(F32)
        marked = (given > 0.5 * MARK) & (row >= 4)
        wanted = jnp.where(marked, given - MARK, ends[0:8])
        value = jnp.where(row < 4, before[8:16], given)
        for step in range(-RIM, RIM + 1):
            if step != 0:
                value = jnp.where(wanted == step, extended[4 + step : 12 + step, :], value)
        operand[c * ROWS : c * ROWS + 16, :] = filled[c * ROWS : c * ROWS + 16, :]
        operand[c * ROWS + 16 : (c + 1) * ROWS, :] = jnp.concatenate([before[0:8], value], axis=0).astype(BF16)
    out[...] = dot(table[...], operand[...], (1, 1)).astype(BF16)


def rows_kernel(spectrum, weight, mirror, following, table, out, by_row, pair):
    tile = lax.axis_index("tile")
    lower = tile < HALF
    last = tile == HALF - 1
    for k in range(4):
        if k < 3:
            own = weight[k + 1 : k + 2]
            other = mirror[7 - k : 8 - k]
        else:
            own = jnp.where(lower, following[0:1], weight[4:5])
            other = jnp.where(lower, mirror[1:2], mirror[4:5])
        both = 0.5 * (own + other)
        if k == 3:
            pair[3:4, :] = jnp.where(last, 0.5 * (mirror[0:1] + mirror[1:2]), both)
            both = jnp.where(last, 0.5 * (following[0:1] + following[1:2]), both)
        else:
            pair[k : k + 1, :] = both
        pair[4 + k : 5 + k, :] = both

    group = lax.broadcasted_iota(jnp.int32, (16, 8, 128), 2) >> 5
    wraps = lax.broadcasted_iota(jnp.int32, (8, 128), 1) >= 128 - RIM
    place = [8 * FIRST_ORDER.index(t) for t in range(TILES)]
    source = spectrum[...].astype(F32)
    source = jnp.concatenate([source[place[t] : place[t] + 8] for t in range(TILES)], axis=0)
    source = source.reshape(4, 4, 4, 8, 2 * 128)
    for half in range(2):
        pieces = []
        for j in range(4):
            piece = source[:, :, j, :, half * 128 : (half + 1) * 128].reshape(128, 128)
            pieces.append([piece if d == 0 else pltpu.roll(piece, 32 * d, 1) for d in range(4)])
        for c in range(4):
            found = pieces[3][(3 - c) % 4].reshape(16, 8, 128)
            for j in range(3):
                found = jnp.where(group == j, pieces[j][(j - c) % 4].reshape(16, 8, 128), found)
            for a in range(4):
                row = FRACTION_ORDER.index(2 * a + half) * 4 + c
                for quarter in range(3):
                    by_row[row, :, quarter * 128 : (quarter + 1) * 128] = found[a * 4 + quarter]
                by_row[row, :, 384:] = jnp.where(wraps, found[(a - 1) % 4 * 4 + 3], found[a * 4 + 3])
    operand = by_row[...].reshape(256, N).astype(BF16)
    scale = pair[...][None]
    with_cosine = dot(operand, table[:, :N], (1, 0)).reshape(32, 8, N) * scale
    with_sine = dot(operand, table[:, N:], (1, 0)).reshape(32, 8, N) * scale
    sign = jnp.where(lax.broadcasted_iota(jnp.int32, (1, 8, 1), 1) < 4, 1.0, -1.0)
    total = with_cosine + sign * pltpu.roll(with_sine, 4, 1)
    out[...] = total.reshape(256, N).astype(BF16)


def back_rows_kernel(parts, spread, table, out, both):
    owned = dot(spread[...], parts[...], (1, 0)).astype(BF16)
    turned = dot(table[...], owned, (1, 1))
    real = turned[:N, :128] - turned[N:, 128:]
    imag = turned[:N, 128:] + turned[N:, :128]
    row = lax.broadcasted_iota(jnp.int32, (TILES, 128), 1) & 7
    for part, value in enumerate((real, imag)):
        picked = value[:TILES]
        for y in range(1, 8):
            picked = jnp.where(row == y, value[y * TILES : (y + 1) * TILES], picked)
        both[pl.ds(part, TILES, stride=2), :] = picked * (1.0 / N)
    out[...] = both[...].astype(BF16)


def back_columns_kernel(spectrum, table, out):
    turned = spectrum[...].astype(F32).T.astype(BF16)
    operand = jnp.concatenate([turned[32 * k : 32 * (k + 1)] for k in range(4)], axis=1)
    image = dot(operand, table[...], (1, 0))
    out[...] = image.reshape(4, 8, N)


def call(kernel, outs, scratch, cost, *args, vmem=None):
    block = pl.BlockSpec(memory_space=pltpu.VMEM)
    blocks = len(args) if vmem is None else vmem
    many = isinstance(outs, (list, tuple))
    return pl.pallas_call(
        kernel,
        out_shape=outs,
        in_specs=[block] * blocks + [pl.BlockSpec(memory_space=pl.ANY)] * (len(args) - blocks),
        out_specs=[block] * len(outs) if many else block,
        scratch_shapes=scratch,
        compiler_params=pltpu.CompilerParams(vmem_limit_bytes=VMEM_LIMIT),
        cost_estimate=pl.CostEstimate(flops=cost, bytes_accessed=1 << 21, transcendentals=0),
    )(*args)


def exchange(blocks, axis, order):
    return lax.all_to_all(blocks, axis, 0, 0, axis_index_groups=[order], tiled=True)


def per_device(frames, gain, defect_pixel, defect_offset, fraction_group, exposure_filter):
    frames = frames.reshape(ROWS, WIDTH)

    shape = jax.ShapeDtypeStruct
    defects = defect_pixel.shape[0]
    def stay(x):
        return pltpu.with_memory_space_constraint(x, pltpu.HBM)

    frames, gain = stay(frames), stay(gain)
    sent, fill_map = call(
        sent_rows_kernel,
        [pltpu.VMEM((8, WIDTH), BF16), pltpu.VMEM((ROWS, WIDTH), BF16)],
        [
            pltpu.VMEM((1, defects), jnp.int32),
            pltpu.VMEM((1, defects), jnp.int32),
            pltpu.VMEM((16, WIDTH), BF16),
            pltpu.VMEM((16, WIDTH), BF16),
            pltpu.VMEM((32, N), F32),
            pltpu.SemaphoreType.DMA((4,)),
        ],
        1 << 27,
        stay(defect_pixel.reshape(1, -1)),
        stay(defect_offset.reshape(1, -1)),
        frames,
        gain,
        vmem=0,
    )
    following_rows = lax.ppermute(sent, "tile", [((t + 1) % TILES, t) for t in range(TILES)])
    filled, tail, weight, mirror, first_rows = call(
        own_rows_kernel,
        [
            pltpu.VMEM((COLS * ROWS, N), BF16),
            pltpu.VMEM((16, WIDTH), BF16),
            pltpu.VMEM((8, N), F32),
            pltpu.VMEM((8, N), F32),
            pltpu.VMEM((2, N), F32),
        ],
        [
            pltpu.SMEM((FRACS,), jnp.int32),
            pltpu.VMEM((8, 8, N), F32),
            pltpu.VMEM((ROWS, WIDTH), BF16),
            pltpu.VMEM((ROWS, WIDTH), BF16),
            pltpu.VMEM((ROWS + 24, N), F32),
            pltpu.SemaphoreType.DMA((4,)),
        ],
        1 << 27,
        fill_map,
        stay(fraction_group),
        stay(exposure_filter),
        frames,
        gain,
        vmem=1,
    )
    mirror = lax.ppermute(mirror, "tile", [(t, TILES - 1 - t) for t in range(TILES)])
    following = lax.ppermute(first_rows, "tile", [((t + 1) % HALF, t) for t in range(HALF)])

    columns = call(
        columns_kernel,
        shape((N, COLS * ROWS), BF16),
        [pltpu.VMEM((16, N), F32), pltpu.VMEM((COLS * ROWS, N), BF16)],
        1 << 27,
        following_rows,
        filled,
        tail,
        jnp.asarray(forward_columns_table()),
    )
    columns = exchange(columns.reshape(TILES, 8, COLS * ROWS), "tile", FIRST_ORDER)

    weighted = call(
        rows_kernel,
        shape((256, N), BF16),
        [pltpu.VMEM((32, 8, N), F32), pltpu.VMEM((8, N), F32)],
        1 << 28,
        columns.reshape(N, COLS * ROWS),
        weight,
        mirror,
        following,
        jnp.asarray(forward_rows_table()),
    )
    parts = exchange(weighted.reshape(FRACS, 32, N), "frac", FRACTION_ORDER)

    back = call(
        back_rows_kernel,
        shape((2 * TILES, 128), BF16),
        [pltpu.VMEM((2 * TILES, 128), F32)],
        1 << 28,
        parts.reshape(256, N),
        jnp.asarray(sum_and_spread_table()),
        jnp.asarray(inverse_rows_table()),
    )
    back = exchange(back.reshape(TILES, 2, 128), "tile", LAST_ORDER)

    return call(
        back_columns_kernel,
        shape((4, 8, N), F32),
        [],
        1 << 26,
        back.reshape(2 * TILES, 128),
        jnp.asarray(inverse_columns_table()),
    )


def solution(mesh):
    return jax.shard_map(
        per_device,
        mesh=mesh,
        in_specs=(
            P("frac", "tile", None),
            P("tile", None),
            P("tile"),
            P("tile"),
            P(),
            P(None, "tile", None),
        ),
        out_specs=P("frac", "tile", None),
        check_vma=False,
    )
```

```python
import jax
import jax.numpy as jnp
import ml_dtypes
import numpy as np
from jax import lax
from jax.experimental import pallas as pl
from jax.experimental.pallas import tpu as pltpu
from jax.sharding import PartitionSpec as P

N = 512
RIM = 4
MARK = 64.0
TILES = 64
HALF = TILES // 2
FIRST_ORDER = [(x + 3) % 4 * 16 + (z + 12) % 16 for x in range(4) for z in range(16)]
FRACTION_ORDER = [(i + 5) % 8 for i in range(8)]
LAST_ORDER = [(x + 2) % 4 * 16 + (z + 8) % 16 for x in range(4) for z in range(16)]
FRACS = 8
COLS = 8
ROWS = 32
WIDTH = N * COLS
F32 = jnp.float32
BF16 = jnp.bfloat16
VMEM_LIMIT = 48 * 1024 * 1024


def wave(a, b):
    angle = (2.0 * np.pi / N) * (np.multiply.outer(a, b) % N)
    return np.cos(angle), np.sin(angle)


def owned_columns():
    tile = np.arange(TILES)[:, None]
    near = np.array([1, 2, 3, 4])[None, :]
    return 8 * tile + np.where(tile < HALF, np.array([1, 2, 3, 8])[None, :], near)


def forward_columns_table():
    cosine, sine = wave(owned_columns(), np.arange(N))
    table = np.stack([cosine, -sine], axis=1)
    table[HALF - 1, 1, 3] = 1.0
    table = table[FIRST_ORDER]
    return table.reshape(N, N).astype(ml_dtypes.bfloat16)


def forward_rows_table():
    cosine, sine = wave((np.arange(N) + RIM) % N, np.arange(N))
    return np.concatenate([cosine, sine], axis=1).astype(ml_dtypes.bfloat16)


def inverse_rows_table():
    rows = (8 * np.array(LAST_ORDER)[None, :] + np.arange(8)[:, None]).reshape(-1)
    cosine, sine = wave(rows, np.arange(N))
    return np.concatenate([cosine, sine], axis=0).astype(ml_dtypes.bfloat16)


def inverse_columns_table():
    cosine, sine = wave(owned_columns(), np.arange(N))
    table = np.stack([2.0 * cosine, -2.0 * sine], axis=1)
    table[HALF - 1, 0, 3] = 1.0 - 2.0 * (np.arange(N) % 2)
    table[HALF - 1, 1, 3] = 1.0
    table = table[LAST_ORDER].transpose(2, 0, 1, 3) / N
    return table.reshape(N, N).astype(ml_dtypes.bfloat16)


def sum_and_spread_table():
    part, k, patch = np.meshgrid(np.arange(2), np.arange(4), np.arange(4), indexing="ij")
    source = (patch * 8 + part * 4 + k).reshape(-1)
    one = np.repeat(source[:, None] == np.arange(32)[None, :], 8, axis=0)
    return np.tile(one, (1, FRACS)).astype(ml_dtypes.bfloat16)


def dot(a, b, contract):
    return lax.dot_general(a, b, ((contract[:1], contract[1:]), ((), ())), preferred_element_type=F32)


def start_copies(pairs, sems):
    copies = [pltpu.make_async_copy(a, b, sems.at[i]) for i, (a, b) in enumerate(pairs)]
    for copy in copies:
        copy.start()
    return copies


def sent_rows_kernel(pixel_in, offset_in, frames_in, gain_in, sent, fill_map, pixel, offset, frames, gain, extended, sems):
    pairs = ((pixel_in, pixel), (offset_in, offset), (frames_in.at[0:16], frames), (gain_in.at[0:16], gain))
    copies = start_copies(pairs, sems)
    copies[0].wait()
    copies[1].wait()
    spot = pixel[...]
    step = offset[...].astype(F32)
    key = ((spot >> 7) & 31) * ROWS + (spot >> 12)
    lane_hot = (lax.broadcasted_iota(jnp.int32, (128, spot.shape[1]), 0) == (spot & 127)).astype(F32).astype(BF16)
    for part in range(4):
        rows = lax.broadcasted_iota(jnp.int32, (256, spot.shape[1]), 0) + 256 * part
        row_hot = jnp.where(rows == key, step, 0.0).astype(BF16)
        found = dot(row_hot, lane_hot, (1, 1)).astype(BF16)
        for i in range(8):
            lane = (part * 8 + i) * 128
            fill_map[:, lane : lane + 128] = found[i * ROWS : (i + 1) * ROWS]
    copies[2].wait()
    copies[3].wait()
    extended[0:8, :] = jnp.zeros((8, N), F32)
    extended[16:24, :] = jnp.zeros((8, N), F32)
    row = lax.broadcasted_iota(jnp.int32, (8, N), 0).astype(F32)
    for c in range(COLS):
        lanes = slice(c * N, (c + 1) * N)
        corrected = (frames[:, lanes].astype(F32) * gain[:, lanes].astype(F32))[0:8]
        extended[8:16, :] = corrected
        wanted = fill_map[0:16, lanes].astype(F32)[0:8]
        value = corrected
        for step in range(-RIM, RIM + 1):
            if step != 0:
                value = jnp.where(wanted == step, extended[8 + step : 16 + step, :], value)
        value = jnp.where(row + wanted < 0.0, MARK + wanted, value)
        extended[24:28, :] = corrected[0:4]
        extended[28:32, :] = value[0:4]
        sent[:, lanes] = extended[24:32, :].astype(BF16)


def own_rows_kernel(fill_map, groups_in, filters_in, frames_in, gain_in, filled, tail, weight, mirror, first_rows, groups, filters, frames, gain, extended, sems):
    pairs = ((groups_in, groups), (filters_in, filters), (frames_in, frames), (gain_in, gain))
    copies = start_copies(pairs, sems)
    turn = (lax.broadcasted_iota(jnp.int32, (N, N), 0) + lax.broadcasted_iota(jnp.int32, (N, N), 1)) & (N - 1)
    turn = (turn == 0).astype(F32).astype(BF16)
    copies[0].wait()
    copies[1].wait()
    square = jnp.zeros(filters.shape[1:], F32)
    for f in range(FRACS):
        square = square + filters[groups[f]] * filters[groups[f]]
    mine = filters[groups[lax.axis_index("frac")]] / jnp.sqrt(square)
    high = mine.astype(BF16)
    low = (mine - high.astype(F32)).astype(BF16)
    back = dot(high, turn, (1, 0)) + dot(low, turn, (1, 0))
    weight[...] = mine
    mirror[...] = back
    mirror[0:1, :] = mine[0:1]
    mirror[1:2, :] = back[0:1]
    first_rows[0:1, :] = mine[0:1]
    first_rows[1:2, :] = back[0:1]

    copies[2].wait()
    copies[3].wait()
    zero = jnp.zeros((8, N), F32)
    row = lax.broadcasted_iota(jnp.int32, (8, N), 0)
    for c in range(COLS):
        lanes = slice(c * N, (c + 1) * N)
        corrected = frames[:, lanes].astype(F32) * gain[:, lanes].astype(F32)
        extended[0:8, :] = zero
        extended[8 : 8 + ROWS, :] = corrected
        extended[8 + ROWS : 16 + ROWS, :] = zero
        wanted = fill_map[:, lanes].astype(F32)
        value = corrected
        for step in range(-RIM, RIM + 1):
            if step != 0:
                value = jnp.where(wanted == step, extended[8 + step : 8 + step + ROWS, :], value)
        late = jnp.where(row.astype(F32) + wanted[ROWS - 8 :] > 7.0, wanted[ROWS - 8 :], 0.0)
        extended[8 : 8 + ROWS, :] = value
        extended[8 + ROWS : 16 + ROWS, :] = late
        late = jnp.where(row < 4, extended[12 + ROWS : 20 + ROWS, :], 0.0)
        tail[:, lanes] = jnp.concatenate([late, corrected[ROWS - 8 :]], axis=0).astype(BF16)
        window = extended[8 + RIM : 8 + RIM + ROWS, :]
        window = jnp.concatenate([window[: ROWS - 8], jnp.where(row < 4, window[ROWS - 8 :], 0.0)], axis=0)
        filled[c * ROWS : (c + 1) * ROWS, :] = window.astype(BF16)


def columns_kernel(following, filled, tail, table, out, extended, operand):
    row = lax.broadcasted_iota(jnp.int32, (8, N), 0)
    for c in range(COLS):
        lanes = slice(c * N, (c + 1) * N)
        given = following[:, lanes].astype(F32)
        ends = tail[:, lanes].astype(F32)
        extended[0:8, :] = ends[8:16]
        extended[8:16, :] = given
        before = filled[c * ROWS + 16 : (c + 1) * ROWS, :].astype(F32)
        marked = (given > 0.5 * MARK) & (row >= 4)
        wanted = jnp.where(marked, given - MARK, ends[0:8])
        value = jnp.where(row < 4, before[8:16], given)
        for step in range(-RIM, RIM + 1):
            if step != 0:
                value = jnp.where(wanted == step, extended[4 + step : 12 + step, :], value)
        operand[c * ROWS : c * ROWS + 16, :] = filled[c * ROWS : c * ROWS + 16, :]
        operand[c * ROWS + 16 : (c + 1) * ROWS, :] = jnp.concatenate([before[0:8], value], axis=0).astype(BF16)
    out[...] = dot(table[...], operand[...], (1, 1)).astype(BF16)


def rows_kernel(spectrum, weight, mirror, following, table, out, by_row, pair):
    tile = lax.axis_index("tile")
    lower = tile < HALF
    last = tile == HALF - 1
    for k in range(4):
        if k < 3:
            own = weight[k + 1 : k + 2]
            other = mirror[7 - k : 8 - k]
        else:
            own = jnp.where(lower, following[0:1], weight[4:5])
            other = jnp.where(lower, mirror[1:2], mirror[4:5])
        both = 0.5 * (own + other)
        if k == 3:
            pair[3:4, :] = jnp.where(last, 0.5 * (mirror[0:1] + mirror[1:2]), both)
            both = jnp.where(last, 0.5 * (following[0:1] + following[1:2]), both)
        else:
            pair[k : k + 1, :] = both
        pair[4 + k : 5 + k, :] = both

    group = lax.broadcasted_iota(jnp.int32, (16, 8, 128), 2) >> 5
    wraps = lax.broadcasted_iota(jnp.int32, (8, 128), 1) >= 128 - RIM
    place = [8 * FIRST_ORDER.index(t) for t in range(TILES)]
    source = spectrum[...].astype(F32)
    source = jnp.concatenate([source[place[t] : place[t] + 8] for t in range(TILES)], axis=0)
    source = source.reshape(4, 4, 4, 8, 2 * 128)
    for half in range(2):
        pieces = []
        for j in range(4):
            piece = source[:, :, j, :, half * 128 : (half + 1) * 128].reshape(128, 128)
            pieces.append([piece if d == 0 else pltpu.roll(piece, 32 * d, 1) for d in range(4)])
        for c in range(4):
            found = pieces[3][(3 - c) % 4].reshape(16, 8, 128)
            for j in range(3):
                found = jnp.where(group == j, pieces[j][(j - c) % 4].reshape(16, 8, 128), found)
            for a in range(4):
                row = FRACTION_ORDER.index(2 * a + half) * 4 + c
                for quarter in range(3):
                    by_row[row, :, quarter * 128 : (quarter + 1) * 128] = found[a * 4 + quarter]
                by_row[row, :, 384:] = jnp.where(wraps, found[(a - 1) % 4 * 4 + 3], found[a * 4 + 3])
    operand = by_row[...].reshape(256, N).astype(BF16)
    scale = pair[...][None]
    with_cosine = dot(operand, table[:, :N], (1, 0)).reshape(32, 8, N) * scale
    with_sine = dot(operand, table[:, N:], (1, 0)).reshape(32, 8, N) * scale
    sign = jnp.where(lax.broadcasted_iota(jnp.int32, (1, 8, 1), 1) < 4, 1.0, -1.0)
    total = with_cosine + sign * pltpu.roll(with_sine, 4, 1)
    out[...] = total.reshape(256, N).astype(BF16)


def back_rows_kernel(parts, spread, table, out, both):
    owned = dot(spread[...], parts[...], (1, 0)).astype(BF16)
    turned = dot(table[...], owned, (1, 1))
    real = turned[:N, :128] - turned[N:, 128:]
    imag = turned[:N, 128:] + turned[N:, :128]
    row = lax.broadcasted_iota(jnp.int32, (TILES, 128), 1) & 7
    for part, value in enumerate((real, imag)):
        picked = value[:TILES]
        for y in range(1, 8):
            picked = jnp.where(row == y, value[y * TILES : (y + 1) * TILES], picked)
        both[pl.ds(part, TILES, stride=2), :] = picked * (1.0 / N)
    out[...] = both[...].astype(BF16)


def back_columns_kernel(spectrum, table, out):
    turned = spectrum[...].astype(F32).T.astype(BF16)
    operand = jnp.concatenate([turned[32 * k : 32 * (k + 1)] for k in range(4)], axis=1)
    image = dot(operand, table[...], (1, 0))
    out[...] = image.reshape(4, 8, N)


def call(kernel, outs, scratch, cost, *args, vmem=None):
    block = pl.BlockSpec(memory_space=pltpu.VMEM)
    blocks = len(args) if vmem is None else vmem
    many = isinstance(outs, (list, tuple))
    return pl.pallas_call(
        kernel,
        out_shape=outs,
        in_specs=[block] * blocks + [pl.BlockSpec(memory_space=pl.ANY)] * (len(args) - blocks),
        out_specs=[block] * len(outs) if many else block,
        scratch_shapes=scratch,
        compiler_params=pltpu.CompilerParams(vmem_limit_bytes=VMEM_LIMIT),
        cost_estimate=pl.CostEstimate(flops=cost, bytes_accessed=1 << 21, transcendentals=0),
    )(*args)


def exchange(blocks, axis, order):
    return lax.all_to_all(blocks, axis, 0, 0, axis_index_groups=[order], tiled=True)


def per_device(frames, gain, defect_pixel, defect_offset, fraction_group, exposure_filter):
    frames = frames.reshape(ROWS, WIDTH)

    shape = jax.ShapeDtypeStruct
    defects = defect_pixel.shape[0]
    def stay(x):
        return pltpu.with_memory_space_constraint(x, pltpu.HBM)

    frames, gain = stay(frames), stay(gain)
    sent, fill_map = call(
        sent_rows_kernel,
        [pltpu.VMEM((8, WIDTH), BF16), pltpu.VMEM((ROWS, WIDTH), BF16)],
        [
            pltpu.VMEM((1, defects), jnp.int32),
            pltpu.VMEM((1, defects), jnp.int32),
            pltpu.VMEM((16, WIDTH), BF16),
            pltpu.VMEM((16, WIDTH), BF16),
            pltpu.VMEM((32, N), F32),
            pltpu.SemaphoreType.DMA((4,)),
        ],
        1 << 27,
        stay(defect_pixel.reshape(1, -1)),
        stay(defect_offset.reshape(1, -1)),
        frames,
        gain,
        vmem=0,
    )
    following_rows = lax.ppermute(sent, "tile", [((t + 1) % TILES, t) for t in range(TILES)])
    filled, tail, weight, mirror, first_rows = call(
        own_rows_kernel,
        [
            pltpu.VMEM((COLS * ROWS, N), BF16),
            pltpu.VMEM((16, WIDTH), BF16),
            pltpu.VMEM((8, N), F32),
            pltpu.VMEM((8, N), F32),
            pltpu.VMEM((2, N), F32),
        ],
        [
            pltpu.SMEM((FRACS,), jnp.int32),
            pltpu.VMEM((8, 8, N), F32),
            pltpu.VMEM((ROWS, WIDTH), BF16),
            pltpu.VMEM((ROWS, WIDTH), BF16),
            pltpu.VMEM((ROWS + 24, N), F32),
            pltpu.SemaphoreType.DMA((4,)),
        ],
        1 << 27,
        fill_map,
        stay(fraction_group),
        stay(exposure_filter),
        frames,
        gain,
        vmem=1,
    )
    mirror = lax.ppermute(mirror, "tile", [(t, TILES - 1 - t) for t in range(TILES)])
    following = lax.ppermute(first_rows, "tile", [((t + 1) % HALF, t) for t in range(HALF)])

    columns = call(
        columns_kernel,
        shape((N, COLS * ROWS), BF16),
        [pltpu.VMEM((16, N), F32), pltpu.VMEM((COLS * ROWS, N), BF16)],
        1 << 27,
        following_rows,
        filled,
        tail,
        jnp.asarray(forward_columns_table()),
    )
    columns = exchange(columns.reshape(TILES, 8, COLS * ROWS), "tile", FIRST_ORDER)

    weighted = call(
        rows_kernel,
        shape((256, N), BF16),
        [pltpu.VMEM((32, 8, N), F32), pltpu.VMEM((8, N), F32)],
        1 << 28,
        columns.reshape(N, COLS * ROWS),
        weight,
        mirror,
        following,
        jnp.asarray(forward_rows_table()),
    )
    parts = exchange(weighted.reshape(FRACS, 32, N), "frac", FRACTION_ORDER)

    back = call(
        back_rows_kernel,
        shape((2 * TILES, 128), BF16),
        [pltpu.VMEM((2 * TILES, 128), F32)],
        1 << 28,
        parts.reshape(256, N),
        jnp.asarray(sum_and_spread_table()),
        jnp.asarray(inverse_rows_table()),
    )
    back = exchange(back.reshape(TILES, 2, 128), "tile", LAST_ORDER)

    return call(
        back_columns_kernel,
        shape((4, 8, N), F32),
        [],
        1 << 26,
        back.reshape(2 * TILES, 128),
        jnp.asarray(inverse_columns_table()),
    )


def solution(mesh):
    return jax.shard_map(
        per_device,
        mesh=mesh,
        in_specs=(
            P("frac", "tile", None),
            P("tile", None),
            P("tile"),
            P("tile"),
            P(),
            P(None, "tile", None),
        ),
        out_specs=P("frac", "tile", None),
        check_vma=False,
    )
```

```python
import jax
import jax.numpy as jnp
import ml_dtypes
import numpy as np
from jax import lax
from jax.experimental import pallas as pl
from jax.experimental.pallas import tpu as pltpu
from jax.sharding import PartitionSpec as P

N = 512
RIM = 4
MARK = 64.0
TILES = 64
HALF = TILES // 2
FIRST_ORDER = [(x + 3) % 4 * 16 + (z + 12) % 16 for x in range(4) for z in range(16)]
FRACTION_ORDER = [(i + 5) % 8 for i in range(8)]
LAST_ORDER = [(x + 2) % 4 * 16 + (z + 8) % 16 for x in range(4) for z in range(16)]
FRACS = 8
COLS = 8
ROWS = 32
WIDTH = N * COLS
F32 = jnp.float32
BF16 = jnp.bfloat16
VMEM_LIMIT = 48 * 1024 * 1024


def wave(a, b):
    angle = (2.0 * np.pi / N) * (np.multiply.outer(a, b) % N)
    return np.cos(angle), np.sin(angle)


def owned_columns():
    tile = np.arange(TILES)[:, None]
    near = np.array([1, 2, 3, 4])[None, :]
    return 8 * tile + np.where(tile < HALF, np.array([1, 2, 3, 8])[None, :], near)


def forward_columns_table():
    cosine, sine = wave(owned_columns(), np.arange(N))
    table = np.stack([cosine, -sine], axis=1)
    table[HALF - 1, 1, 3] = 1.0
    table = table[FIRST_ORDER]
    return table.reshape(N, N).astype(ml_dtypes.bfloat16)


def forward_rows_table():
    cosine, sine = wave((np.arange(N) + RIM) % N, np.arange(N))
    return np.concatenate([cosine, sine], axis=1).astype(ml_dtypes.bfloat16)


def inverse_rows_table():
    rows = (8 * np.array(LAST_ORDER)[None, :] + np.arange(8)[:, None]).reshape(-1)
    cosine, sine = wave(rows, np.arange(N))
    return np.concatenate([cosine, sine], axis=0).astype(ml_dtypes.bfloat16)


def inverse_columns_table():
    cosine, sine = wave(owned_columns(), np.arange(N))
    table = np.stack([2.0 * cosine, -2.0 * sine], axis=1)
    table[HALF - 1, 0, 3] = 1.0 - 2.0 * (np.arange(N) % 2)
    table[HALF - 1, 1, 3] = 1.0
    table = table[LAST_ORDER].transpose(2, 0, 1, 3) / N
    return table.reshape(N, N).astype(ml_dtypes.bfloat16)


def sum_and_spread_table():
    part, k, patch = np.meshgrid(np.arange(2), np.arange(4), np.arange(4), indexing="ij")
    source = (patch * 8 + part * 4 + k).reshape(-1)
    one = np.repeat(source[:, None] == np.arange(32)[None, :], 8, axis=0)
    return np.tile(one, (1, FRACS)).astype(ml_dtypes.bfloat16)


def dot(a, b, contract):
    return lax.dot_general(a, b, ((contract[:1], contract[1:]), ((), ())), preferred_element_type=F32)


def start_copies(pairs, sems):
    copies = [pltpu.make_async_copy(a, b, sems.at[i]) for i, (a, b) in enumerate(pairs)]
    for copy in copies:
        copy.start()
    return copies


def sent_rows_kernel(pixel_in, offset_in, frames_in, gain_in, sent, fill_map, pixel, offset, frames, gain, extended, sems):
    pairs = ((pixel_in, pixel), (offset_in, offset), (frames_in.at[0:16], frames), (gain_in.at[0:16], gain))
    copies = start_copies(pairs, sems)
    copies[0].wait()
    copies[1].wait()
    spot = pixel[...]
    step = offset[...].astype(F32)
    key = ((spot >> 7) & 31) * ROWS + (spot >> 12)
    lane_hot = (lax.broadcasted_iota(jnp.int32, (128, spot.shape[1]), 0) == (spot & 127)).astype(F32).astype(BF16)
    for part in range(4):
        rows = lax.broadcasted_iota(jnp.int32, (256, spot.shape[1]), 0) + 256 * part
        row_hot = jnp.where(rows == key, step, 0.0).astype(BF16)
        found = dot(row_hot, lane_hot, (1, 1)).astype(BF16)
        for i in range(8):
            lane = (part * 8 + i) * 128
            fill_map[:, lane : lane + 128] = found[i * ROWS : (i + 1) * ROWS]
    copies[2].wait()
    copies[3].wait()
    extended[0:8, :] = jnp.zeros((8, N), F32)
    extended[16:24, :] = jnp.zeros((8, N), F32)
    row = lax.broadcasted_iota(jnp.int32, (8, N), 0).astype(F32)
    for c in range(COLS):
        lanes = slice(c * N, (c + 1) * N)
        corrected = (frames[:, lanes].astype(F32) * gain[:, lanes].astype(F32))[0:8]
        extended[8:16, :] = corrected
        wanted = fill_map[0:16, lanes].astype(F32)[0:8]
        value = corrected
        for step in range(-RIM, RIM + 1):
            if step != 0:
                value = jnp.where(wanted == step, extended[8 + step : 16 + step, :], value)
        value = jnp.where(row + wanted < 0.0, MARK + wanted, value)
        extended[24:28, :] = corrected[0:4]
        extended[28:32, :] = value[0:4]
        sent[:, lanes] = extended[24:32, :].astype(BF16)


def own_rows_kernel(fill_map, groups_in, filters_in, frames_in, gain_in, filled, tail, weight, mirror, first_rows, groups, filters, frames, gain, extended, sems):
    pairs = ((groups_in, groups), (filters_in, filters), (frames_in, frames), (gain_in, gain))
    copies = start_copies(pairs, sems)
    turn = (lax.broadcasted_iota(jnp.int32, (N, N), 0) + lax.broadcasted_iota(jnp.int32, (N, N), 1)) & (N - 1)
    turn = (turn == 0).astype(F32).astype(BF16)
    copies[0].wait()
    copies[1].wait()
    square = jnp.zeros(filters.shape[1:], F32)
    for f in range(FRACS):
        square = square + filters[groups[f]] * filters[groups[f]]
    mine = filters[groups[lax.axis_index("frac")]] / jnp.sqrt(square)
    high = mine.astype(BF16)
    low = (mine - high.astype(F32)).astype(BF16)
    back = dot(high, turn, (1, 0)) + dot(low, turn, (1, 0))
    weight[...] = mine
    mirror[...] = back
    mirror[0:1, :] = mine[0:1]
    mirror[1:2, :] = back[0:1]
    first_rows[0:1, :] = mine[0:1]
    first_rows[1:2, :] = back[0:1]

    copies[2].wait()
    copies[3].wait()
    zero = jnp.zeros((8, N), F32)
    row = lax.broadcasted_iota(jnp.int32, (8, N), 0)
    for c in range(COLS):
        lanes = slice(c * N, (c + 1) * N)
        corrected = frames[:, lanes].astype(F32) * gain[:, lanes].astype(F32)
        extended[0:8, :] = zero
        extended[8 : 8 + ROWS, :] = corrected
        extended[8 + ROWS : 16 + ROWS, :] = zero
        wanted = fill_map[:, lanes].astype(F32)
        value = corrected
        for step in range(-RIM, RIM + 1):
            if step != 0:
                value = jnp.where(wanted == step, extended[8 + step : 8 + step + ROWS, :], value)
        late = jnp.where(row.astype(F32) + wanted[ROWS - 8 :] > 7.0, wanted[ROWS - 8 :], 0.0)
        extended[8 : 8 + ROWS, :] = value
        extended[8 + ROWS : 16 + ROWS, :] = late
        late = jnp.where(row < 4, extended[12 + ROWS : 20 + ROWS, :], 0.0)
        tail[:, lanes] = jnp.concatenate([late, corrected[ROWS - 8 :]], axis=0).astype(BF16)
        window = extended[8 + RIM : 8 + RIM + ROWS, :]
        window = jnp.concatenate([window[: ROWS - 8], jnp.where(row < 4, window[ROWS - 8 :], 0.0)], axis=0)
        filled[c * ROWS : (c + 1) * ROWS, :] = window.astype(BF16)


def columns_kernel(following, filled, tail, table, out, extended, operand):
    row = lax.broadcasted_iota(jnp.int32, (8, N), 0)
    for c in range(COLS):
        lanes = slice(c * N, (c + 1) * N)
        given = following[:, lanes].astype(F32)
        ends = tail[:, lanes].astype(F32)
        extended[0:8, :] = ends[8:16]
        extended[8:16, :] = given
        before = filled[c * ROWS + 16 : (c + 1) * ROWS, :].astype(F32)
        marked = (given > 0.5 * MARK) & (row >= 4)
        wanted = jnp.where(marked, given - MARK, ends[0:8])
        value = jnp.where(row < 4, before[8:16], given)
        for step in range(-RIM, RIM + 1):
            if step != 0:
                value = jnp.where(wanted == step, extended[4 + step : 12 + step, :], value)
        operand[c * ROWS : c * ROWS + 16, :] = filled[c * ROWS : c * ROWS + 16, :]
        operand[c * ROWS + 16 : (c + 1) * ROWS, :] = jnp.concatenate([before[0:8], value], axis=0).astype(BF16)
    out[...] = dot(table[...], operand[...], (1, 1)).astype(BF16)


def rows_kernel(spectrum, weight, mirror, following, table, out, by_row, pair):
    tile = lax.axis_index("tile")
    lower = tile < HALF
    last = tile == HALF - 1
    for k in range(4):
        if k < 3:
            own = weight[k + 1 : k + 2]
            other = mirror[7 - k : 8 - k]
        else:
            own = jnp.where(lower, following[0:1], weight[4:5])
            other = jnp.where(lower, mirror[1:2], mirror[4:5])
        both = 0.5 * (own + other)
        if k == 3:
            pair[3:4, :] = jnp.where(last, 0.5 * (mirror[0:1] + mirror[1:2]), both)
            both = jnp.where(last, 0.5 * (following[0:1] + following[1:2]), both)
        else:
            pair[k : k + 1, :] = both
        pair[4 + k : 5 + k, :] = both

    group = lax.broadcasted_iota(jnp.int32, (16, 8, 128), 2) >> 5
    wraps = lax.broadcasted_iota(jnp.int32, (8, 128), 1) >= 128 - RIM
    place = [8 * FIRST_ORDER.index(t) for t in range(TILES)]
    source = spectrum[...].astype(F32)
    source = jnp.concatenate([source[place[t] : place[t] + 8] for t in range(TILES)], axis=0)
    source = source.reshape(4, 4, 4, 8, 2 * 128)
    for half in range(2):
        pieces = []
        for j in range(4):
            piece = source[:, :, j, :, half * 128 : (half + 1) * 128].reshape(128, 128)
            pieces.append([piece if d == 0 else pltpu.roll(piece, 32 * d, 1) for d in range(4)])
        for c in range(4):
            found = pieces[3][(3 - c) % 4].reshape(16, 8, 128)
            for j in range(3):
                found = jnp.where(group == j, pieces[j][(j - c) % 4].reshape(16, 8, 128), found)
            for a in range(4):
                row = FRACTION_ORDER.index(2 * a + half) * 4 + c
                for quarter in range(3):
                    by_row[row, :, quarter * 128 : (quarter + 1) * 128] = found[a * 4 + quarter]
                by_row[row, :, 384:] = jnp.where(wraps, found[(a - 1) % 4 * 4 + 3], found[a * 4 + 3])
    operand = by_row[...].reshape(256, N).astype(BF16)
    scale = pair[...][None]
    signed = jnp.where(lax.broadcasted_iota(jnp.int32, (1, 8, 1), 1) < 4, -scale, scale)
    with_cosine = dot(operand, table[:, :N], (1, 0)).reshape(32, 8, N) * scale
    with_sine = dot(operand, table[:, N:], (1, 0)).reshape(32, 8, N) * signed
    total = with_cosine + pltpu.roll(with_sine, 4, 1)
    out[...] = total.reshape(256, N).astype(BF16)


def back_rows_kernel(parts, spread, table, out, both):
    owned = dot(spread[...], parts[...], (1, 0)).astype(BF16)
    turned = dot(table[...], owned, (1, 1))
    real = turned[:N, :128] - turned[N:, 128:]
    imag = turned[:N, 128:] + turned[N:, :128]
    row = lax.broadcasted_iota(jnp.int32, (TILES, 128), 1) & 7
    for part, value in enumerate((real, imag)):
        picked = value[:TILES]
        for y in range(1, 8):
            picked = jnp.where(row == y, value[y * TILES : (y + 1) * TILES], picked)
        both[pl.ds(part, TILES, stride=2), :] = picked * (1.0 / N)
    out[...] = both[...].astype(BF16)


def back_columns_kernel(spectrum, table, out):
    turned = spectrum[...].astype(F32).T.astype(BF16)
    operand = jnp.concatenate([turned[32 * k : 32 * (k + 1)] for k in range(4)], axis=1)
    image = dot(operand, table[...], (1, 0))
    out[...] = image.reshape(4, 8, N)


def call(kernel, outs, scratch, cost, *args, vmem=None):
    block = pl.BlockSpec(memory_space=pltpu.VMEM)
    blocks = len(args) if vmem is None else vmem
    many = isinstance(outs, (list, tuple))
    return pl.pallas_call(
        kernel,
        out_shape=outs,
        in_specs=[block] * blocks + [pl.BlockSpec(memory_space=pl.ANY)] * (len(args) - blocks),
        out_specs=[block] * len(outs) if many else block,
        scratch_shapes=scratch,
        compiler_params=pltpu.CompilerParams(vmem_limit_bytes=VMEM_LIMIT),
        cost_estimate=pl.CostEstimate(flops=cost, bytes_accessed=1 << 21, transcendentals=0),
    )(*args)


def exchange(blocks, axis, order):
    return lax.all_to_all(blocks, axis, 0, 0, axis_index_groups=[order], tiled=True)


def per_device(frames, gain, defect_pixel, defect_offset, fraction_group, exposure_filter):
    frames = frames.reshape(ROWS, WIDTH)

    shape = jax.ShapeDtypeStruct
    defects = defect_pixel.shape[0]
    def stay(x):
        return pltpu.with_memory_space_constraint(x, pltpu.HBM)

    frames, gain = stay(frames), stay(gain)
    sent, fill_map = call(
        sent_rows_kernel,
        [pltpu.VMEM((8, WIDTH), BF16), pltpu.VMEM((ROWS, WIDTH), BF16)],
        [
            pltpu.VMEM((1, defects), jnp.int32),
            pltpu.VMEM((1, defects), jnp.int32),
            pltpu.VMEM((16, WIDTH), BF16),
            pltpu.VMEM((16, WIDTH), BF16),
            pltpu.VMEM((32, N), F32),
            pltpu.SemaphoreType.DMA((4,)),
        ],
        1 << 27,
        stay(defect_pixel.reshape(1, -1)),
        stay(defect_offset.reshape(1, -1)),
        frames,
        gain,
        vmem=0,
    )
    following_rows = lax.ppermute(sent, "tile", [((t + 1) % TILES, t) for t in range(TILES)])
    filled, tail, weight, mirror, first_rows = call(
        own_rows_kernel,
        [
            pltpu.VMEM((COLS * ROWS, N), BF16),
            pltpu.VMEM((16, WIDTH), BF16),
            pltpu.VMEM((8, N), F32),
            pltpu.VMEM((8, N), F32),
            pltpu.VMEM((2, N), F32),
        ],
        [
            pltpu.SMEM((FRACS,), jnp.int32),
            pltpu.VMEM((8, 8, N), F32),
            pltpu.VMEM((ROWS, WIDTH), BF16),
            pltpu.VMEM((ROWS, WIDTH), BF16),
            pltpu.VMEM((ROWS + 24, N), F32),
            pltpu.SemaphoreType.DMA((4,)),
        ],
        1 << 27,
        fill_map,
        stay(fraction_group),
        stay(exposure_filter),
        frames,
        gain,
        vmem=1,
    )
    mirror = lax.ppermute(mirror, "tile", [(t, TILES - 1 - t) for t in range(TILES)])
    following = lax.ppermute(first_rows, "tile", [((t + 1) % HALF, t) for t in range(HALF)])

    columns = call(
        columns_kernel,
        shape((N, COLS * ROWS), BF16),
        [pltpu.VMEM((16, N), F32), pltpu.VMEM((COLS * ROWS, N), BF16)],
        1 << 27,
        following_rows,
        filled,
        tail,
        jnp.asarray(forward_columns_table()),
    )
    columns = exchange(columns.reshape(TILES, 8, COLS * ROWS), "tile", FIRST_ORDER)

    weighted = call(
        rows_kernel,
        shape((256, N), BF16),
        [pltpu.VMEM((32, 8, N), F32), pltpu.VMEM((8, N), F32)],
        1 << 28,
        columns.reshape(N, COLS * ROWS),
        weight,
        mirror,
        following,
        jnp.asarray(forward_rows_table()),
    )
    parts = exchange(weighted.reshape(FRACS, 32, N), "frac", FRACTION_ORDER)

    back = call(
        back_rows_kernel,
        shape((2 * TILES, 128), BF16),
        [pltpu.VMEM((2 * TILES, 128), F32)],
        1 << 28,
        parts.reshape(256, N),
        jnp.asarray(sum_and_spread_table()),
        jnp.asarray(inverse_rows_table()),
    )
    back = exchange(back.reshape(TILES, 2, 128), "tile", LAST_ORDER)

    return call(
        back_columns_kernel,
        shape((4, 8, N), F32),
        [],
        1 << 26,
        back.reshape(2 * TILES, 128),
        jnp.asarray(inverse_columns_table()),
    )


def solution(mesh):
    return jax.shard_map(
        per_device,
        mesh=mesh,
        in_specs=(
            P("frac", "tile", None),
            P("tile", None),
            P("tile"),
            P("tile"),
            P(),
            P(None, "tile", None),
        ),
        out_specs=P("frac", "tile", None),
        check_vma=False,
    )
```
